32 devices in a mesh: cross: 2 (over core), strike: 16 (over z, y, x).
Axes of the slice: x: 2, y: 2, z: 4, core: 2. Of those that a mesh axis runs over, the one named last changes fastest.
Arguments:
- pressure: float32 [1024, 2, 2048], P('strike', 'cross'), may hold values from -6 to 6
- source: float32 [1024, 2, 2048], P('strike', 'cross'), may hold values from -6 to 6
- facies: int32 [1024, 2, 2048], P('strike', 'cross'), may hold values from 0 to 7
- mobility_table: float32 [8], replicated, may hold values from 0.3 to 3
Outputs:
- pressure_out: float32 [1024, 2, 2048], P('strike', 'cross')
- defect: float32 [1024, 2, 2048], P('strike', 'cross')
The draws below stay inside these ranges and needn't reach their ends.
All inputs are finite; a program needn't handle non-finite values.
Results may differ from the reference program's by a relative error of at most 0.0003.
Values sent between devices are 32-bit elements; how exact they have to be, the bound alone decides.
A program may use at most 64 MiB of HBM per device.

```python
import math
import jax
import jax.numpy as jnp
from jax import lax

ND = 1024
CLASSES = 8
DEFECT = 2
SWEEPS = 3
NC = 2
NS = 2048


def place_ends(array, own_key, least, high):
    extent = array.shape
    place = [jax.random.randint(jax.random.fold_in(own_key, axis), (), 0, extent[axis]) for axis in range(len(extent))]
    array = array.at[tuple(place)].set(least)
    longest = extent.index(max(extent))
    place[longest] = (place[longest] + 1) % extent[longest]
    return array.at[tuple(place)].set(high)


def block_levels(rng, extent, split, smallest, largest):
    gain = 1.0
    for dim, blocks in split:
        heights = jax.random.uniform(jax.random.fold_in(jax.random.fold_in(rng, 6), dim), (blocks,), jnp.float32, smallest / len(split), largest / len(split))
        gain = gain * jnp.repeat(jnp.exp(heights), extent[dim] // blocks).reshape((-1,) + (1,) * (len(extent) - 1 - dim))
    return gain


def centred(rng, extent, scale, bound, shards=(), kind=jnp.bfloat16):
    entries = scale * jax.random.normal(rng, extent, jnp.float32)
    if shards:
        entries = entries * block_levels(rng, extent, shards, -0.22, 0.18)
    return jnp.clip(entries, -bound, bound).astype(kind)


def setup_inputs(seed: int = 0) -> dict:
    key_of = jax.random.split(jax.random.key(seed), 5)
    pressure = centred(key_of[0], (ND, NC, NS), 1.0, 6.0, ((0, 16), (1, 2)), jnp.float32)
    source = centred(key_of[1], (ND, NC, NS), 1.0, 6.0, ((0, 16), (1, 2)), jnp.float32)
    facies = place_ends(jax.random.randint(key_of[2], (ND, NC, NS), 0, CLASSES), jax.random.fold_in(key_of[2], 1), 0, CLASSES - 1).astype(jnp.int32)
    mobility_table = jnp.clip(jnp.exp(jax.random.uniform(key_of[3], (CLASSES,), jnp.float32, math.log(0.3), math.log(3.0))), 0.3, 3.0)
    return dict(pressure=pressure, source=source, facies=facies, mobility_table=mobility_table)


STORE = 0.5
LOW = 0.05
HIGH = 1.95

def chebyshev_weights(count):
    middle = 0.5 * (LOW + HIGH)
    half = 0.5 * (HIGH - LOW)
    return [1.0 / (middle + half * math.cos(math.pi * (2 * j + 1) / (2 * count))) for j in range(count)]

def neighbour(padded, axis, offset, shape):
    starts = [1, 1, 1]
    starts[axis] = offset
    limits = [s + n for s, n in zip(starts, shape)]
    return lax.slice(padded, starts, limits)

def operate_padded(field, mobile, padded_f, padded_m):
    total = STORE * field
    for axis in range(3):
        for offset in (0, 2):
            near_f = neighbour(padded_f, axis, offset, field.shape)
            near_m = neighbour(padded_m, axis, offset, field.shape)
            total = total + 0.5 * (mobile + near_m) * (field - near_f)
    return total

def lookup(classes, table):
    base = jnp.zeros(classes.shape, table.dtype)
    for code in range(CLASSES):
        base = jnp.where(classes == code, table[code], base)
    return base

def forward_plane(plane):
    count = plane.shape[0]
    whole = jnp.concatenate([plane, plane[::-1]], axis=0)
    spectrum = jnp.fft.fft(whole, axis=0)[:count]
    wave = jnp.arange(count).astype(plane.dtype)
    twist = jnp.exp(-1j * jnp.pi * wave / (2 * count))
    scale = jnp.where(wave == 0, jnp.sqrt(1.0 / count), jnp.sqrt(2.0 / count)).astype(plane.dtype)
    return (scale[:, None] * 0.5 * jnp.real(twist[:, None] * spectrum)).astype(plane.dtype)

def inverse_plane(coeffs):
    count = coeffs.shape[0]
    wave = jnp.arange(count).astype(coeffs.dtype)
    twist = jnp.exp(1j * jnp.pi * wave / (2 * count))
    scale = jnp.where(wave == 0, jnp.sqrt(1.0 / count), jnp.sqrt(2.0 / count)).astype(coeffs.dtype)
    spread = scale[:, None] * coeffs * twist[:, None]
    padded = jnp.concatenate([spread, jnp.zeros_like(spread)], axis=0)
    values = jnp.fft.ifft(padded, axis=0) * (2 * count)
    return jnp.real(values[:count]).astype(coeffs.dtype)

def along_dip(function, field):
    planes = jnp.moveaxis(field, 1, 0)
    return jnp.moveaxis(lax.map(function, planes), 0, 1)

def plane_sweeps(rhat, mref):
    count = rhat.shape[0]
    omega = chebyshev_weights(SWEEPS)
    lam = (2.0 - 2.0 * jnp.cos(jnp.pi * jnp.arange(count).astype(rhat.dtype) / count))[:, None, None]
    diag = STORE + mref * (lam + 4.0)
    answer = omega[0] * rhat / diag
    for step in range(1, SWEEPS):
        padded = jnp.pad(answer, ((0, 0), (1, 1), (1, 1)))
        near = padded[:, :-2, 1:-1] + padded[:, 2:, 1:-1] + padded[:, 1:-1, :-2] + padded[:, 1:-1, 2:]
        answer = answer + omega[step] * (rhat - (diag * answer - mref * near)) / diag
    return answer

def reference(pressure, source, facies, mobility_table):
    base = lookup(facies, mobility_table)
    field = pressure
    defect = jnp.zeros_like(pressure)
    for step in range(DEFECT):
        mobile = base * (1.0 + 0.5 * jnp.tanh(field))
        residual = source - operate_padded(field, mobile, jnp.pad(field, 1), jnp.pad(mobile, 1))
        defect = residual
        rhat = along_dip(forward_plane, residual)
        mref = lax.optimization_barrier(jnp.mean(mobile, axis=0, keepdims=True))
        answer = plane_sweeps(rhat, mref)
        field = field + along_dip(inverse_plane, answer)
    return (field, defect)
```

```python
import functools
import math

import jax
import jax.numpy as jnp
from jax import lax
from jax.experimental import pallas as pl
from jax.experimental.pallas import tpu as pltpu
from jax.sharding import PartitionSpec as P

CLASSES = 8
DEFECT = 2
SWEEPS = 3

STORE = 0.5
LOW = 0.05
HIGH = 1.95

SUB = 8
LANES = 128
HALF = LANES // 2
MESH = pl.DeviceIdType.MESH


def chebyshev_weights(count):
    middle = 0.5 * (LOW + HIGH)
    half = 0.5 * (HIGH - LOW)
    return [
        1.0 / (middle + half * math.cos(math.pi * (2 * j + 1) / (2 * count))) for j in range(count)
    ]


def lookup(classes, table):
    base = jnp.zeros(classes.shape, jnp.float32)
    for code in range(CLASSES):
        base = jnp.where(classes == code, table[code], base)
    return base


def power(x, count):
    result = None
    while count:
        if count & 1:
            result = x if result is None else result * x
        count >>= 1
        if count:
            x = x * x
    return result


def group_size(count):
    low = 1
    while low * low < count:
        low *= 2
    return low if count % low == 0 else count


def kernel(
    crosses, strikes, dips, xin, out, x, rims, mob, res, ans, part, qpow, col, rim_ans, rim_base,
    near_box, far_box, cross_sems, own_sem, rim_sems, near_sems, far_sems, out_sems, out_own,
):
    tiles, width = x.shape[2], x.shape[4]
    main = width - LANES
    rows = tiles * SUB
    members = near_box.shape[1]
    groups = far_box.shape[1]
    cross = lax.axis_index("cross")
    strike = lax.axis_index("strike")
    member = lax.rem(strike, members)
    group = lax.div(strike, members)

    def across(k):
        return lax.rem(cross + k, crosses)

    def before(k):
        return lax.rem(cross + crosses - k, crosses)

    up = lax.rem(strike + 1, strikes)
    down = lax.rem(strike + strikes - 1, strikes)

    def near_peer(k):
        return (cross, group * members + lax.rem(member + k, members))

    def far_peer(k):
        return (cross, lax.rem(group + k, groups) * members + member)

    barrier = pltpu.get_barrier_semaphore()
    peers = [(across(k), strike) for k in range(1, crosses)]
    peers += [(across(k), side) for k in range(crosses) for side in (up, down)]
    peers += [near_peer(k) for k in range(1, members)]
    peers += [far_peer(k) for k in range(1, groups)]
    for peer in peers:
        pl.semaphore_signal(barrier, inc=1, device_id=peer, device_id_type=MESH)
    pl.semaphore_wait(barrier, len(peers))

    own = pltpu.make_async_copy(xin.at[cross], x.at[cross], own_sem)
    own.start()
    rim_copies = []
    for k in range(crosses):
        for side, target, tile, row in ((0, up, tiles - 1, SUB - 1), (1, down, 0, 0)):
            rim_copies.append(
                pltpu.make_async_remote_copy(
                    src_ref=xin.at[across(k), pl.ds(0, 2), tile, pl.ds(row, 1), :],
                    dst_ref=rims.at[side, cross],
                    send_sem=rim_sems.at[0, side, k],
                    recv_sem=rim_sems.at[1, side, k],
                    device_id=(across(k), target),
                    device_id_type=MESH,
                )
            )
    cross_copies = [
        pltpu.make_async_remote_copy(
            src_ref=xin.at[across(k)],
            dst_ref=x.at[cross],
            send_sem=cross_sems.at[0, k - 1],
            recv_sem=cross_sems.at[1, k - 1],
            device_id=(across(k), strike),
            device_id_type=MESH,
        )
        for k in range(1, crosses)
    ]
    for copy in cross_copies + rim_copies:
        copy.start()
    own.wait()
    for k in range(1, crosses):
        pltpu.make_async_remote_copy(
            src_ref=x.at[before(k)],
            dst_ref=x.at[before(k)],
            send_sem=cross_sems.at[0, k - 1],
            recv_sem=cross_sems.at[1, k - 1],
            device_id=(across(k), strike),
            device_id_type=MESH,
        ).wait_recv()
    for k in range(crosses):
        for side, target in ((0, up), (1, down)):
            pltpu.make_async_remote_copy(
                src_ref=rims.at[side, before(k)],
                dst_ref=rims.at[side, before(k)],
                send_sem=rim_sems.at[0, side, k],
                recv_sem=rim_sems.at[1, side, k],
                device_id=(across(k), target),
                device_id_type=MESH,
            ).wait_recv()
    for copy in cross_copies + rim_copies:
        copy.wait_send()

    inside = (strike > 0, strike < strikes - 1)
    lane = lax.broadcasted_iota(jnp.int32, (1, 1, width), 2)
    valid = (
        (lane < main)
        | ((lane < main + HALF) & (cross < crosses - 1))
        | ((lane >= main + HALF) & (cross > 0))
    )
    sub = lax.broadcasted_iota(jnp.int32, (crosses, SUB, width), 1)
    none = jnp.zeros((1, SUB, width), jnp.float32)

    for side in range(2):
        rim_ans[side, 1] = jnp.where(inside[side], rims[side, :, 0], 0.0)
        rim_base[side] = jnp.where(inside[side], rims[side, :, 1], 0.0)

    def left(a):
        return pltpu.roll(a, 1, 2)

    def right(a):
        return pltpu.roll(a, width - 1, 2)

    def later(a, k):
        return pltpu.roll(a, k, 1)

    def sooner(a, k):
        return pltpu.roll(a, SUB - k, 1)

    def mobility(base, p):
        return base * (1.0 + 0.5 * jnp.tanh(p))

    def trade(box, sems, slot, count, peer_of, mine, parity):
        box[parity, mine] = slot
        copies = []
        for k in range(1, count):
            copy = pltpu.make_async_remote_copy(
                src_ref=box.at[parity, mine],
                dst_ref=box.at[parity, mine],
                send_sem=sems.at[0, parity, k - 1],
                recv_sem=sems.at[1, parity, k - 1],
                device_id=peer_of(k),
                device_id_type=MESH,
            )
            copy.start()
            copies.append(copy)

        def finish():
            for k in range(1, count):
                origin = lax.rem(mine + count - k, count)
                pltpu.make_async_remote_copy(
                    src_ref=box.at[parity, origin],
                    dst_ref=box.at[parity, origin],
                    send_sem=sems.at[0, parity, k - 1],
                    recv_sem=sems.at[1, parity, k - 1],
                    device_id=peer_of(k),
                    device_id_type=MESH,
                ).wait_recv()
            for copy in copies:
                copy.wait_send()

        return finish

    def trade_near(slot, parity):
        return trade(near_box, near_sems, slot, members, near_peer, member, parity)

    def trade_far(slot, parity):
        return trade(far_box, far_sems, slot, groups, far_peer, group, parity)

    omega = chebyshev_weights(SWEEPS)

    def one_step(step, carry):
        turn = step * (SWEEPS + 1)
        parity = lax.rem(turn, 2)
        total = jnp.zeros((crosses, SUB, width), jnp.float32)
        for t in range(tiles):
            m = mobility(x[:, 1, t], x[:, 0, t])
            mob[t] = m
            total = total + m
        total = jnp.sum(total, axis=1, keepdims=True)
        finish = trade_near(jnp.stack([total, total]), parity)

        rim_p = [rim_ans[side, 1] for side in range(2)]
        rim_m = [mobility(rim_base[side], rim_p[side]) for side in range(2)]
        first_p, first_m = x[:, 0, 0], mob[0]
        last_p, last_m = x[:, 0, tiles - 1], mob[tiles - 1]
        p_was = jnp.where(sub == 0, rim_p[0], later(last_p, 1))
        m_was = jnp.where(sub == 0, rim_m[0], later(last_m, 1))
        p, m = first_p, first_m
        flux = 0.5 * (m + m_was) * (p - p_was)
        for t in range(tiles):
            if t + 1 < tiles:
                p_next, m_next = x[:, 0, t + 1], mob[t + 1]
            else:
                p_next = jnp.where(sub == SUB - 1, rim_p[1], sooner(first_p, 1))
                m_next = jnp.where(sub == SUB - 1, rim_m[1], sooner(first_m, 1))
            flux_next = 0.5 * (m_next + m) * (p_next - p)
            along = 0.5 * (m + left(m)) * (p - left(p))
            p_wide = jnp.concatenate([none, p, none], axis=0)
            m_wide = jnp.concatenate([none, m, none], axis=0)
            over = 0.5 * (m_wide[1:] + m_wide[:-1]) * (p_wide[1:] - p_wide[:-1])
            applied = STORE * p + (flux - flux_next) + (along - right(along)) + (over[:-1] - over[1:])
            res[:, t] = jnp.where(valid, x[:, 2, t] - applied, 0.0)
            ans[t] = jnp.zeros_like(p)
            p, m, flux = p_next, m_next, flux_next

        finish()
        total = near_box[parity, 0, 0]
        for a in range(1, members):
            total = total + near_box[parity, a, 0]
        trade_far(jnp.stack([total, total]), parity)()
        total = far_box[parity, 0, 0]
        for a in range(1, groups):
            total = total + far_box[parity, a, 0]
        mref = total * (1.0 / dips)

        root = jnp.sqrt((STORE + 4.0 * mref) * (STORE + 8.0 * mref))
        q = 2.0 * mref / (STORE + 6.0 * mref + root)
        gain = 1.0 / root
        chunk = power(q, tiles)
        block = power(q, rows)
        cluster = power(block, members)
        whole = power(cluster, groups)
        unmirror = 1.0 / (1.0 - whole * whole)
        col[0], col[1], col[2], col[3], col[4], col[5], col[6], col[7] = (
            mref, q, gain, chunk, block, cluster, whole, unmirror
        )
        running = q
        for t in range(tiles):
            qpow[t] = running
            running = running * q
        ahead = jnp.ones((crosses, SUB, width), jnp.float32)
        behind = ahead
        step_up = jnp.broadcast_to(chunk, ahead.shape)
        for bit in (1, 2, 4):
            ahead = jnp.where((sub & bit) != 0, ahead * step_up, ahead)
            behind = jnp.where((sub & bit) == 0, behind * step_up, behind)
            step_up = step_up * step_up
        part[0], part[1] = ahead, behind
        for side in range(2):
            rim_ans[side, 0] = jnp.zeros((crosses, 1, width), jnp.float32)

        def sweep(j, carry):
            parity = lax.rem(turn + 1 + j, 2)
            weight = jnp.float32(omega[0])
            for i in range(1, SWEEPS):
                weight = jnp.where(j == i, jnp.float32(omega[i]), weight)
            keep = 1.0 - weight
            mref, q, chunk = col[0], col[1], col[3]

            y = jnp.zeros((crosses, SUB, width), jnp.float32)
            for t in range(tiles):
                u = ans[t]
                near = left(u) + right(u)
                if crosses > 1:
                    near = near + jnp.concatenate([none, u[:-1]], axis=0)
                    near = near + jnp.concatenate([u[1:], none], axis=0)
                r = res[:, t] + mref * near
                mob[t] = r
                y = r + q * y
                qv = y - r
                part[2 + t] = qv
            z = jnp.zeros((crosses, SUB, width), jnp.float32)
            for t in reversed(range(tiles)):
                z = mob[t] + q * z
                part[2 + t] = part[2 + t] + z
            step_up = chunk
            for k in (1, 2, 4):
                y = y + step_up * jnp.where(sub >= k, later(y, k), 0.0)
                z = z + step_up * jnp.where(sub < SUB - k, sooner(z, k), 0.0)
                step_up = step_up * step_up
            tail, head = y[:, SUB - 1 :, :], z[:, :1, :]
            trade_near(jnp.stack([tail, head]), parity)()

            block, cluster, whole, unmirror = col[4], col[5], col[6], col[7]
            fore = near_box[parity, 0, 0]
            back = near_box[parity, members - 1, 1]
            for a in range(1, members):
                fore = fore * block + near_box[parity, a, 0]
                back = back * block + near_box[parity, members - 1 - a, 1]
            trade_far(jnp.stack([fore, back]), parity)()
            fore = far_box[parity, 0, 0]
            back = far_box[parity, groups - 1, 1]
            for a in range(1, groups):
                fore = fore * cluster + far_box[parity, a, 0]
                back = back * cluster + far_box[parity, groups - 1 - a, 1]
            from_left = (back + whole * fore) * unmirror
            from_right = (fore + whole * back) * unmirror
            for a in range(groups - 1):
                b = groups - 1 - a
                from_left = jnp.where(
                    a < group, from_left * cluster + far_box[parity, a, 0], from_left
                )
                from_right = jnp.where(
                    b > group, from_right * cluster + far_box[parity, b, 1], from_right
                )
            for a in range(members - 1):
                b = members - 1 - a
                from_left = jnp.where(
                    a < member, from_left * block + near_box[parity, a, 0], from_left
                )
                from_right = jnp.where(
                    b > member, from_right * block + near_box[parity, b, 1], from_right
                )

            scale = weight * col[2]
            rim_ans[0, 0] = keep * rim_ans[0, 0] + scale * (
                from_left + q * (head + block * from_right)
            )
            rim_ans[1, 0] = keep * rim_ans[1, 0] + scale * (
                from_right + q * (tail + block * from_left)
            )
            y = jnp.where(sub >= 1, later(y, 1), 0.0) + part[0] * from_left
            z = jnp.where(sub < SUB - 1, sooner(z, 1), 0.0) + part[1] * from_right
            for t in range(tiles):
                solved = part[2 + t] + qpow[t] * y + qpow[tiles - 1 - t] * z
                ans[t] = keep * ans[t] + scale * solved
            return carry

        lax.fori_loop(0, SWEEPS, sweep, 0)
        for t in range(tiles):
            x[:, 0, t] = x[:, 0, t] + ans[t]
        for side in range(2):
            rim_ans[side, 1] = rim_ans[side, 1] + jnp.where(inside[side], rim_ans[side, 0], 0.0)
        return carry

    lax.fori_loop(0, DEFECT, one_step, 0)

    keeps = [
        pltpu.make_async_copy(x.at[cross, 0, :, :, pl.ds(0, main)], out.at[0, cross], out_own.at[0]),
        pltpu.make_async_copy(res.at[cross, :, :, pl.ds(0, main)], out.at[1, cross], out_own.at[1]),
    ]
    gives = []
    for k in range(1, crosses):
        for which in range(2):
            source = x.at[across(k), 0] if which == 0 else res.at[across(k)]
            gives.append(
                pltpu.make_async_remote_copy(
                    src_ref=source.at[:, :, pl.ds(0, main)],
                    dst_ref=out.at[which, cross],
                    send_sem=out_sems.at[0, which, k - 1],
                    recv_sem=out_sems.at[1, which, k - 1],
                    device_id=(across(k), strike),
                    device_id_type=MESH,
                )
            )
    for copy in gives + keeps:
        copy.start()
    for copy in keeps:
        copy.wait()
    for k in range(1, crosses):
        for which in range(2):
            pltpu.make_async_remote_copy(
                src_ref=out.at[which, before(k)],
                dst_ref=out.at[which, before(k)],
                send_sem=out_sems.at[0, which, k - 1],
                recv_sem=out_sems.at[1, which, k - 1],
                device_id=(across(k), strike),
                device_id_type=MESH,
            ).wait_recv()
    for copy in gives:
        copy.wait_send()


def per_device(pressure, source, facies, mobility_table):
    crosses = lax.axis_size("cross")
    strikes = lax.axis_size("strike")
    rows, _, cells = pressure.shape
    tiles = rows // SUB
    main = cells // crosses
    width = main + LANES
    members = group_size(strikes)
    groups = strikes // members

    base = lookup(facies, mobility_table)

    def dealt(a):
        return a.reshape(SUB, tiles, cells).transpose(1, 0, 2)

    whole = jnp.stack([dealt(pressure), dealt(base), dealt(source)])
    empty = jnp.zeros(whole.shape[:-1] + (LANES,), jnp.float32)
    low = lax.broadcasted_iota(jnp.int32, empty.shape, 3) < HALF
    windows = []
    for k in range(crosses):
        after = whole[..., (k + 1) * main : (k + 1) * main + LANES] if k + 1 < crosses else empty
        ahead = whole[..., k * main - LANES : k * main] if k > 0 else empty
        windows.append(
            jnp.concatenate(
                [whole[..., k * main : (k + 1) * main], jnp.where(low, after, ahead)], axis=-1
            )
        )
    xin = jnp.stack(windows)

    f32 = jnp.float32
    vm = pltpu.VMEM
    dma = pltpu.SemaphoreType.DMA
    field = (tiles, crosses, SUB, width)
    thin = (crosses, 1, width)
    out = pl.pallas_call(
        functools.partial(kernel, crosses, strikes, rows * strikes),
        out_shape=jax.ShapeDtypeStruct((2, crosses, tiles, SUB, main), f32),
        in_specs=[pl.BlockSpec(memory_space=pl.ANY)],
        out_specs=pl.BlockSpec(memory_space=pl.ANY),
        scratch_shapes=[
            vm((crosses, 3, tiles, SUB, width), f32),
            vm((2, crosses, 2, 1, width), f32),
            vm(field, f32),
            vm((crosses, tiles, SUB, width), f32),
            vm(field, f32),
            vm((tiles + 2,) + field[1:], f32),
            vm((tiles,) + thin, f32),
            vm((8,) + thin, f32),
            vm((2, 2) + thin, f32),
            vm((2,) + thin, f32),
            vm((2, members, 2) + thin, f32),
            vm((2, groups, 2) + thin, f32),
            dma((2, max(crosses - 1, 1))),
            dma,
            dma((2, 2, crosses)),
            dma((2, 2, max(members - 1, 1))),
            dma((2, 2, max(groups - 1, 1))),
            dma((2, 2, max(crosses - 1, 1))),
            dma((2,)),
        ],
        compiler_params=pltpu.CompilerParams(
            collective_id=0, has_side_effects=True, vmem_limit_bytes=40 * 1024 * 1024
        ),
    )(xin)

    def gathered(a):
        return a.transpose(2, 1, 0, 3).reshape(rows, 1, cells)

    return gathered(out[0]), gathered(out[1])


def solution(mesh):
    in_specs = (
        P("strike", "cross", None),
        P("strike", "cross", None),
        P("strike", "cross", None),
        P(),
    )
    out_specs = (P("strike", "cross", None), P("strike", "cross", None))
    return jax.shard_map(
        per_device, mesh=mesh, in_specs=in_specs, out_specs=out_specs, check_vma=False
    )
```

```python
import functools
import math

import jax
import jax.numpy as jnp
from jax import lax
from jax.experimental import pallas as pl
from jax.experimental.pallas import tpu as pltpu
from jax.sharding import PartitionSpec as P

CLASSES = 8
DEFECT = 2
SWEEPS = 3

STORE = 0.5
LOW = 0.05
HIGH = 1.95

SUB = 8
LANES = 128
HALF = LANES // 2
MESH = pl.DeviceIdType.MESH


def chebyshev_weights(count):
    middle = 0.5 * (LOW + HIGH)
    half = 0.5 * (HIGH - LOW)
    return [
        1.0 / (middle + half * math.cos(math.pi * (2 * j + 1) / (2 * count))) for j in range(count)
    ]


def power(x, count):
    result = None
    while count:
        if count & 1:
            result = x if result is None else result * x
        count >>= 1
        if count:
            x = x * x
    return result


def group_size(count):
    low = 1
    while low * low < count:
        low *= 2
    return low if count % low == 0 else count


def kernel(
    crosses, strikes, dips, pressure, facies, source, table, out_p, out_d, x, fac, halo, halo_fac,
    rims, mob, res, ans, part, qpow, full, col, rim_ans, rim_base, near_box, far_box, far_out,
    cross_sems, halo_sems, rim_sems, near_sems, far_sems, out_sems,
):
    tiles, width = x.shape[2], x.shape[4]
    main = width - LANES
    rows = tiles * SUB
    members = near_box.shape[1]
    groups = far_box.shape[1]
    cross = lax.axis_index("cross")
    strike = lax.axis_index("strike")
    member = lax.rem(strike, members)
    group = lax.div(strike, members)

    def across(k):
        return lax.rem(cross + k, crosses)

    def before(k):
        return lax.rem(cross + crosses - k, crosses)

    up = lax.rem(strike + 1, strikes)
    down = lax.rem(strike + strikes - 1, strikes)

    def near_peer(k):
        return (cross, group * members + lax.rem(member + k, members))

    def far_peer(k):
        return (cross, lax.rem(group + k, groups) * members + member)

    barrier = pltpu.get_barrier_semaphore()
    peers = [(across(k), strike) for k in range(1, crosses)]
    peers += [(cross, up), (cross, down)]
    peers += [near_peer(k) for k in range(1, members)]
    peers += [far_peer(k) for k in range(1, groups)]
    for peer in peers:
        pl.semaphore_signal(barrier, inc=1, device_id=peer, device_id_type=MESH)
    pl.semaphore_wait(barrier, len(peers))

    def send(src, dst, sems, where, target, k):
        if k == 0:
            return pltpu.make_async_copy(src, dst, sems.at[(1,) + where])
        return pltpu.make_async_remote_copy(
            src_ref=src,
            dst_ref=dst,
            send_sem=sems.at[(0,) + where],
            recv_sem=sems.at[(1,) + where],
            device_id=target,
            device_id_type=MESH,
        )

    def arrived(ref, sems, where, target, k):
        copy = send(ref, ref, sems, where, target, k)
        if k == 0:
            copy.wait()
        else:
            copy.wait_recv()

    def landing(f, c):
        if f == 1:
            return fac.at[c, :, :, pl.ds(0, main)], halo_fac.at[c]
        return x.at[c, f, :, :, pl.ds(0, main)], halo.at[c, f // 2]

    def columns(start, size):
        return pl.ds(pl.multiple_of(start, LANES), size)

    raws = (pressure, facies, source)
    for k in range(crosses):
        to = across(k)
        after = lax.rem(to + 1, crosses) * main
        ahead = lax.rem(to + crosses - 1, crosses) * main + main - LANES
        for f in range(3):
            body, edge = landing(f, cross)
            for t in range(tiles):
                send(
                    raws[f].at[:, t, 0, columns(to * main, main)], body.at[t],
                    cross_sems, (f, k), (to, strike), k,
                ).start()
            for t in range(tiles):
                for side, begin in ((0, after), (1, ahead)):
                    send(
                        raws[f].at[:, t, 0, columns(begin, LANES)], edge.at[side, t],
                        halo_sems, (f, k), (to, strike), k,
                    ).start()
    for k in range(crosses):
        for f in range(3):
            body, edge = landing(f, before(k))
            arrived(body, cross_sems, (f, k), (across(k), strike), k)
            arrived(edge, halo_sems, (f, k), (across(k), strike), k)

    inside = (strike > 0, strike < strikes - 1)
    lane = lax.broadcasted_iota(jnp.int32, (1, 1, width), 2)
    valid = (
        (lane < main)
        | ((lane < main + HALF) & (cross < crosses - 1))
        | ((lane >= main + HALF) & (cross > 0))
    )
    sub = lax.broadcasted_iota(jnp.int32, (crosses, SUB, width), 1)
    none = jnp.zeros((1, SUB, width), jnp.float32)
    tip = lax.broadcasted_iota(jnp.int32, (crosses, SUB, LANES), 2) < HALF
    real = valid[:, :, main:]

    def classed(codes):
        base = jnp.zeros(codes.shape, jnp.float32)
        for code in range(CLASSES):
            base = jnp.where(codes == code, table[code], base)
        return base

    for t in range(tiles):
        for f in (0, 2):
            merged = jnp.where(tip, halo[:, f // 2, 0, t], halo[:, f // 2, 1, t])
            x[:, f, t, :, main:] = jnp.where(real, merged, 0.0)
        merged = classed(jnp.where(tip, halo_fac[:, 0, t], halo_fac[:, 1, t]))
        x[:, 1, t, :, main:] = jnp.where(real, merged, 0.0)
        x[:, 1, t, :, :main] = classed(fac[:, t, :, :main])

    rim_copies = [
        send(
            x.at[:, pl.ds(0, 2), tile, pl.ds(row, 1), :], rims.at[side],
            rim_sems, (side,), (cross, target), 1,
        )
        for side, target, tile, row in ((0, up, tiles - 1, SUB - 1), (1, down, 0, 0))
    ]
    for copy in rim_copies:
        copy.start()

    def finals(which):
        ref = out_p if which == 0 else out_d
        copies = []
        for k in range(crosses):
            to = across(k)
            for t in range(tiles):
                src = x.at[to, 0, t] if which == 0 else res.at[to, t]
                copies.append(
                    send(
                        src.at[:, pl.ds(0, main)],
                        ref.at[:, t, 0, columns(cross * main, main)],
                        out_sems, (which, k), (to, strike), k,
                    )
                )
        return copies

    def left(a):
        return pltpu.roll(a, 1, 2)

    def right(a):
        return pltpu.roll(a, width - 1, 2)

    def later(a, k):
        return pltpu.roll(a, k, 1)

    def sooner(a, k):
        return pltpu.roll(a, SUB - k, 1)

    def mobility(base, p):
        return base * (1.0 + 0.5 * jnp.tanh(p))

    def trade(source, box, sems, count, peer_of, mine, parity):
        copies = []
        for k in range(1, count):
            copy = send(
                source(k), box(mine), sems, (parity, k - 1), peer_of(k), k
            )
            copy.start()
            copies.append(copy)

        def finish():
            for k in range(1, count):
                origin = lax.rem(mine + count - k, count)
                arrived(box(origin), sems, (parity, k - 1), peer_of(k), k)
            for copy in copies:
                copy.wait_send()

        return finish

    def trade_near(slots, parity):
        for i, slot in enumerate(slots):
            near_box[parity, member, i] = slot

        def box(a):
            return near_box.at[parity, a, pl.ds(0, len(slots))]

        return trade(lambda k: box(member), box, near_sems, members, near_peer, member, parity)

    def trade_far(upward, downward, parity):
        far_out[parity, 0] = upward
        far_out[parity, 1] = downward
        return trade(
            lambda k: far_out.at[parity, lax.div(group + k, groups)],
            lambda a: far_box.at[parity, a],
            far_sems, groups, far_peer, group, parity,
        )

    omega = chebyshev_weights(SWEEPS)

    def one_step(step, carry):
        turn = step * (SWEEPS + 1)
        parity = lax.rem(turn, 2)
        total = jnp.zeros((crosses, SUB, width), jnp.float32)
        for t in range(tiles):
            m = mobility(x[:, 1, t], x[:, 0, t])
            mob[t] = m
            total = total + m
        total = jnp.sum(total, axis=1, keepdims=True)
        finish = trade_near([total], parity)

        @pl.when(step == 0)
        def _():
            for copy in rim_copies:
                copy.wait_recv()
            for copy in rim_copies:
                copy.wait_send()
            for side in range(2):
                rim_ans[side, 1] = jnp.where(inside[side], rims[side, :, 0], 0.0)
                rim_base[side] = jnp.where(inside[side], rims[side, :, 1], 0.0)

        rim_p = [rim_ans[side, 1] for side in range(2)]
        rim_m = [mobility(rim_base[side], rim_p[side]) for side in range(2)]
        first_p, first_m = x[:, 0, 0], mob[0]
        last_p, last_m = x[:, 0, tiles - 1], mob[tiles - 1]
        p_was = jnp.where(sub == 0, rim_p[0], later(last_p, 1))
        m_was = jnp.where(sub == 0, rim_m[0], later(last_m, 1))
        p, m = first_p, first_m
        flux = 0.5 * (m + m_was) * (p - p_was)
        for t in range(tiles):
            if t + 1 < tiles:
                p_next, m_next = x[:, 0, t + 1], mob[t + 1]
            else:
                p_next = jnp.where(sub == SUB - 1, rim_p[1], sooner(first_p, 1))
                m_next = jnp.where(sub == SUB - 1, rim_m[1], sooner(first_m, 1))
            flux_next = 0.5 * (m_next + m) * (p_next - p)
            along = 0.5 * (m + left(m)) * (p - left(p))
            p_wide = jnp.concatenate([none, p, none], axis=0)
            m_wide = jnp.concatenate([none, m, none], axis=0)
            over = 0.5 * (m_wide[1:] + m_wide[:-1]) * (p_wide[1:] - p_wide[:-1])
            applied = STORE * p + (flux - flux_next) + (along - right(along)) + (over[:-1] - over[1:])
            res[:, t] = jnp.where(valid, x[:, 2, t] - applied, 0.0)
            ans[t] = jnp.zeros_like(p)
            p, m, flux = p_next, m_next, flux_next
            if t == tiles // 2 - 1:
                finish()
                total = near_box[parity, 0, 0]
                for a in range(1, members):
                    total = total + near_box[parity, a, 0]
                far_box[parity, group] = total
                finish = trade_far(total, total, parity)

        @pl.when(step == DEFECT - 1)
        def _():
            for copy in finals(1):
                copy.start()

        finish()
        total = far_box[parity, 0]
        for a in range(1, groups):
            total = total + far_box[parity, a]
        mref = total * (1.0 / dips)

        root = jnp.sqrt((STORE + 4.0 * mref) * (STORE + 8.0 * mref))
        q = 2.0 * mref / (STORE + 6.0 * mref + root)
        gain = 1.0 / root
        chunk = power(q, tiles)
        block = power(q, rows)
        cluster = power(block, members)
        whole = power(cluster, groups)
        unmirror = 1.0 / (1.0 - whole * whole)
        mirror_up = jnp.ones_like(q)
        mirror_down = mirror_up
        twice = cluster * cluster
        for a in range(groups - 1):
            mirror_up = jnp.where(a < group, mirror_up * twice, mirror_up)
            mirror_down = jnp.where(a < groups - 1 - group, mirror_down * twice, mirror_down)
        for i, value in enumerate((chunk, block, cluster, unmirror, mirror_up, mirror_down)):
            col[i] = value
        spread = (crosses, SUB, width)
        for i, value in enumerate((mref, q, gain)):
            full[i] = jnp.broadcast_to(value, spread)
        running = q
        for t in range(tiles):
            qpow[t] = jnp.broadcast_to(running, spread)
            running = running * q
        ahead = jnp.ones((crosses, SUB, width), jnp.float32)
        behind = ahead
        step_up = jnp.broadcast_to(chunk, ahead.shape)
        for bit in (1, 2, 4):
            ahead = jnp.where((sub & bit) != 0, ahead * step_up, ahead)
            behind = jnp.where((sub & bit) == 0, behind * step_up, behind)
            step_up = step_up * step_up
        part[0], part[1] = ahead, behind
        for side in range(2):
            rim_ans[side, 0] = jnp.zeros((crosses, 1, width), jnp.float32)

        def sweep(j, carry):
            parity = lax.rem(turn + 1 + j, 2)
            weight = jnp.float32(omega[0])
            for i in range(1, SWEEPS):
                weight = jnp.where(j == i, jnp.float32(omega[i]), weight)
            keep = 1.0 - weight
            mref, q, chunk = full[0], full[1], col[0]

            y = jnp.zeros((crosses, SUB, width), jnp.float32)
            for t in range(tiles):
                u = ans[t]
                near = left(u) + right(u)
                if crosses > 1:
                    near = near + jnp.concatenate([none, u[:-1]], axis=0)
                    near = near + jnp.concatenate([u[1:], none], axis=0)
                r = res[:, t] + mref * near
                mob[t] = r
                y = r + q * y
                qv = y - r
                part[2 + t] = qv
            z = jnp.zeros((crosses, SUB, width), jnp.float32)
            for t in reversed(range(tiles)):
                z = mob[t] + q * z
                part[2 + t] = part[2 + t] + z
            step_up = chunk
            for k in (1, 2, 4):
                y = y + step_up * jnp.where(sub >= k, later(y, k), 0.0)
                z = z + step_up * jnp.where(sub < SUB - k, sooner(z, k), 0.0)
                step_up = step_up * step_up
            tail, head = y[:, SUB - 1 :, :], z[:, :1, :]
            trade_near([tail, head], parity)()

            block, cluster, unmirror = col[1], col[2], col[3]
            fore = near_box[parity, 0, 0]
            back = near_box[parity, members - 1, 1]
            for a in range(1, members):
                fore = fore * block + near_box[parity, a, 0]
                back = back * block + near_box[parity, members - 1 - a, 1]
            mirror_up, mirror_down = col[4], col[5]
            upward = fore + mirror_up * cluster * back
            downward = back + mirror_down * cluster * fore
            trade_far(upward, downward, parity)()
            from_left = jnp.zeros_like(upward)
            from_right = jnp.zeros_like(upward)
            for a in range(groups - 1):
                b = groups - 1 - a
                from_left = jnp.where(
                    a < group, from_left * cluster + far_box[parity, a], from_left
                )
                from_right = jnp.where(
                    b > group, from_right * cluster + far_box[parity, b], from_right
                )
            from_left, from_right = (
                (from_left + mirror_up * (from_right * cluster + downward)) * unmirror,
                (from_right + mirror_down * (from_left * cluster + upward)) * unmirror,
            )
            for a in range(members - 1):
                b = members - 1 - a
                from_left = jnp.where(
                    a < member, from_left * block + near_box[parity, a, 0], from_left
                )
                from_right = jnp.where(
                    b > member, from_right * block + near_box[parity, b, 1], from_right
                )

            thin_q = q[:, :1, :]
            scale = weight * full[2]
            thin_scale = scale[:, :1, :]
            rim_ans[0, 0] = keep * rim_ans[0, 0] + thin_scale * (
                from_left + thin_q * (head + block * from_right)
            )
            rim_ans[1, 0] = keep * rim_ans[1, 0] + thin_scale * (
                from_right + thin_q * (tail + block * from_left)
            )
            y = jnp.where(sub >= 1, later(y, 1), 0.0) + part[0] * from_left
            z = jnp.where(sub < SUB - 1, sooner(z, 1), 0.0) + part[1] * from_right
            for t in range(tiles):
                solved = part[2 + t] + qpow[t] * y + qpow[tiles - 1 - t] * z
                ans[t] = keep * ans[t] + scale * solved
            return carry

        lax.fori_loop(0, SWEEPS, sweep, 0)
        for t in range(tiles):
            x[:, 0, t] = x[:, 0, t] + ans[t]
        for side in range(2):
            rim_ans[side, 1] = rim_ans[side, 1] + jnp.where(inside[side], rim_ans[side, 0], 0.0)
        return carry

    lax.fori_loop(0, DEFECT, one_step, 0)

    for copy in finals(0):
        copy.start()
    for which in (1, 0):
        ref = out_p if which == 0 else out_d
        for k in range(crosses):
            to, frm = across(k), before(k)
            arrived(
                ref.at[:, :, 0, columns(frm * main, main)], out_sems, (which, k), (to, strike), k
            )
    for k in range(1, crosses):
        to = across(k)
        for f in range(3):
            body, edge = landing(f, cross)
            send(body, body, cross_sems, (f, k), (to, strike), k).wait_send()
            send(edge, edge, halo_sems, (f, k), (to, strike), k).wait_send()
        for which in range(2):
            src = x.at[to, 0] if which == 0 else res.at[to]
            src = src.at[:, :, pl.ds(0, main)]
            send(src, src, out_sems, (which, k), (to, strike), k).wait_send()


def per_device(pressure, source, facies, mobility_table):
    crosses = lax.axis_size("cross")
    strikes = lax.axis_size("strike")
    rows, _, cells = pressure.shape
    tiles = rows // SUB
    main = cells // crosses
    width = main + LANES
    members = group_size(strikes)
    groups = strikes // members

    def dealt(a):
        return a.reshape(SUB, tiles, 1, cells)

    f32 = jnp.float32
    vm = pltpu.VMEM
    dma = pltpu.SemaphoreType.DMA
    full = (crosses, SUB, width)
    field = (tiles,) + full
    thin = (crosses, 1, width)
    whole = jax.ShapeDtypeStruct((SUB, tiles, 1, cells), f32)
    anywhere = pl.BlockSpec(memory_space=pl.ANY)
    outs = pl.pallas_call(
        functools.partial(kernel, crosses, strikes, rows * strikes),
        out_shape=[whole, whole],
        in_specs=[anywhere] * 3 + [pl.BlockSpec(memory_space=pltpu.SMEM)],
        out_specs=[anywhere] * 2,
        scratch_shapes=[
            vm((crosses, 3, tiles, SUB, width), f32),
            vm((crosses, tiles, SUB, width), jnp.int32),
            vm((crosses, 2, 2, tiles, SUB, LANES), f32),
            vm((crosses, 2, tiles, SUB, LANES), jnp.int32),
            vm((2, crosses, 2, 1, width), f32),
            vm(field, f32),
            vm((crosses, tiles, SUB, width), f32),
            vm(field, f32),
            vm((tiles + 2,) + full, f32),
            vm(field, f32),
            vm((3,) + full, f32),
            vm((6,) + thin, f32),
            vm((2, 2) + thin, f32),
            vm((2,) + thin, f32),
            vm((2, members, 2) + thin, f32),
            vm((2, groups) + thin, f32),
            vm((2, 2) + thin, f32),
            dma((2, 3, crosses)),
            dma((2, 3, crosses)),
            dma((2, 2)),
            dma((2, 2, max(members - 1, 1))),
            dma((2, 2, max(groups - 1, 1))),
            dma((2, 2, crosses)),
        ],
        compiler_params=pltpu.CompilerParams(
            collective_id=0, has_side_effects=True, vmem_limit_bytes=40 * 1024 * 1024
        ),
    )(dealt(pressure), dealt(facies), dealt(source), mobility_table)
    return tuple(a.reshape(rows, 1, cells) for a in outs)


def solution(mesh):
    in_specs = (
        P("strike", "cross", None),
        P("strike", "cross", None),
        P("strike", "cross", None),
        P(),
    )
    out_specs = (P("strike", "cross", None), P("strike", "cross", None))
    return jax.shard_map(
        per_device, mesh=mesh, in_specs=in_specs, out_specs=out_specs, check_vma=False
    )
```

```python
import functools
import math

import jax
import jax.numpy as jnp
from jax import lax
from jax.experimental import pallas as pl
from jax.experimental.pallas import tpu as pltpu
from jax.sharding import PartitionSpec as P

CLASSES = 8
DEFECT = 2
SWEEPS = 3

STORE = 0.5
LOW = 0.05
HIGH = 1.95

SUB = 8
LANES = 128
HALF = LANES // 2
MESH = pl.DeviceIdType.MESH


def chebyshev_weights(count):
    middle = 0.5 * (LOW + HIGH)
    half = 0.5 * (HIGH - LOW)
    return [
        1.0 / (middle + half * math.cos(math.pi * (2 * j + 1) / (2 * count))) for j in range(count)
    ]


def power(x, count):
    result = None
    while count:
        if count & 1:
            result = x if result is None else result * x
        count >>= 1
        if count:
            x = x * x
    return result


def kernel(
    crosses, strikes, dips, pressure, facies, source, table, out_p, out_d, x, fac, halo, halo_fac,
    rims, mob, res, ans, part, qpow, full, col, rim_ans, rim_base, near_box, far_box, far_out,
    cross_sems, halo_sems, rim_sems, near_sems, far_sems, out_sems,
):
    tiles, width = x.shape[2], x.shape[4]
    main = width - LANES
    rows = tiles * SUB
    members = near_box.shape[1]
    groups = far_box.shape[1]
    cross = lax.axis_index("cross")
    strike = lax.axis_index("strike")
    member = lax.rem(strike, members)
    group = lax.div(strike, members)

    def across(k):
        return lax.rem(cross + k, crosses)

    def before(k):
        return lax.rem(cross + crosses - k, crosses)

    up = lax.rem(strike + 1, strikes)
    down = lax.rem(strike + strikes - 1, strikes)

    def near_peer(k):
        return (cross, group * members + lax.rem(member + k, members))

    def far_peer(k):
        return (cross, lax.rem(group + k, groups) * members + member)

    barrier = pltpu.get_barrier_semaphore()
    peers = [(across(k), strike) for k in range(1, crosses)]
    peers += [(cross, up), (cross, down)]
    peers += [near_peer(k) for k in range(1, members)]
    peers += [far_peer(k) for k in range(1, groups)]
    for peer in peers:
        pl.semaphore_signal(barrier, inc=1, device_id=peer, device_id_type=MESH)
    pl.semaphore_wait(barrier, len(peers))

    def send(src, dst, sems, where, target, k):
        if k == 0:
            return pltpu.make_async_copy(src, dst, sems.at[(1,) + where])
        return pltpu.make_async_remote_copy(
            src_ref=src,
            dst_ref=dst,
            send_sem=sems.at[(0,) + where],
            recv_sem=sems.at[(1,) + where],
            device_id=target,
            device_id_type=MESH,
        )

    def arrived(ref, sems, where, target, k):
        copy = send(ref, ref, sems, where, target, k)
        if k == 0:
            copy.wait()
        else:
            copy.wait_recv()

    def landing(f, c):
        if f == 1:
            return fac.at[c, :, :, pl.ds(0, main)], halo_fac.at[c]
        return x.at[c, f, :, :, pl.ds(0, main)], halo.at[c, f // 2]

    def columns(start, size):
        return pl.ds(pl.multiple_of(start, LANES), size)

    raws = (pressure, facies, source)
    for k in range(crosses):
        to = across(k)
        after = lax.rem(to + 1, crosses) * main
        ahead = lax.rem(to + crosses - 1, crosses) * main + main - LANES
        for f in range(3):
            body, edge = landing(f, cross)
            for t in range(tiles):
                send(
                    raws[f].at[:, t, 0, columns(to * main, main)], body.at[t],
                    cross_sems, (f, k), (to, strike), k,
                ).start()
            for t in range(tiles):
                for side, begin in ((0, after), (1, ahead)):
                    send(
                        raws[f].at[:, t, 0, columns(begin, LANES)], edge.at[side, t],
                        halo_sems, (f, k), (to, strike), k,
                    ).start()
    for k in range(crosses):
        for f in range(3):
            body, edge = landing(f, before(k))
            arrived(body, cross_sems, (f, k), (across(k), strike), k)
            arrived(edge, halo_sems, (f, k), (across(k), strike), k)

    inside = (strike > 0, strike < strikes - 1)
    lane = lax.broadcasted_iota(jnp.int32, (1, 1, width), 2)
    valid = (
        (lane < main)
        | ((lane < main + HALF) & (cross < crosses - 1))
        | ((lane >= main + HALF) & (cross > 0))
    )
    sub = lax.broadcasted_iota(jnp.int32, (crosses, SUB, width), 1)
    none = jnp.zeros((1, SUB, width), jnp.float32)
    tip = lax.broadcasted_iota(jnp.int32, (crosses, SUB, LANES), 2) < HALF
    real = valid[:, :, main:]

    def classed(codes):
        base = jnp.zeros(codes.shape, jnp.float32)
        for code in range(CLASSES):
            base = jnp.where(codes == code, table[code], base)
        return base

    for t in range(tiles):
        for f in (0, 2):
            merged = jnp.where(tip, halo[:, f // 2, 0, t], halo[:, f // 2, 1, t])
            x[:, f, t, :, main:] = jnp.where(real, merged, 0.0)
        merged = classed(jnp.where(tip, halo_fac[:, 0, t], halo_fac[:, 1, t]))
        x[:, 1, t, :, main:] = jnp.where(real, merged, 0.0)
        x[:, 1, t, :, :main] = classed(fac[:, t, :, :main])

    rim_copies = [
        send(
            x.at[:, pl.ds(0, 2), tile, pl.ds(row, 1), :], rims.at[side],
            rim_sems, (side,), (cross, target), 1,
        )
        for side, target, tile, row in ((0, up, tiles - 1, SUB - 1), (1, down, 0, 0))
    ]
    for copy in rim_copies:
        copy.start()

    def finals(which):
        ref = out_p if which == 0 else out_d
        copies = []
        for k in range(crosses):
            to = across(k)
            for t in range(tiles):
                src = x.at[to, 0, t] if which == 0 else res.at[to, t]
                copies.append(
                    send(
                        src.at[:, pl.ds(0, main)],
                        ref.at[:, t, 0, columns(cross * main, main)],
                        out_sems, (which, k), (to, strike), k,
                    )
                )
        return copies

    def left(a):
        return pltpu.roll(a, 1, 2)

    def right(a):
        return pltpu.roll(a, width - 1, 2)

    def later(a, k):
        return pltpu.roll(a, k, 1)

    def sooner(a, k):
        return pltpu.roll(a, SUB - k, 1)

    def mobility(base, p):
        return base * (1.0 + 0.5 * jnp.tanh(p))

    def trade(source, box, sems, count, peer_of, mine, parity):
        copies = []
        for k in range(1, count):
            copy = send(
                source(k), box(mine), sems, (parity, k - 1), peer_of(k), k
            )
            copy.start()
            copies.append(copy)

        def finish():
            for k in range(1, count):
                origin = lax.rem(mine + count - k, count)
                arrived(box(origin), sems, (parity, k - 1), peer_of(k), k)
            for copy in copies:
                copy.wait_send()

        return finish

    def trade_near(slots, parity):
        for i, slot in enumerate(slots):
            near_box[parity, member, i] = slot

        def box(a):
            return near_box.at[parity, a, pl.ds(0, len(slots))]

        return trade(lambda k: box(member), box, near_sems, members, near_peer, member, parity)

    def trade_far(upward, downward, parity):
        far_out[parity, 0] = upward
        far_out[parity, 1] = downward
        return trade(
            lambda k: far_out.at[parity, lax.div(group + k, groups)],
            lambda a: far_box.at[parity, a],
            far_sems, groups, far_peer, group, parity,
        )

    omega = chebyshev_weights(SWEEPS)

    def one_step(step, carry):
        turn = step * (SWEEPS + 1)
        parity = lax.rem(turn, 2)
        total = jnp.zeros((crosses, SUB, width), jnp.float32)
        for t in range(tiles):
            m = mobility(x[:, 1, t], x[:, 0, t])
            mob[t] = m
            total = total + m
        total = jnp.sum(total, axis=1, keepdims=True)
        finish = trade_near([total], parity)

        @pl.when(step == 0)
        def _():
            for copy in rim_copies:
                copy.wait_recv()
            for copy in rim_copies:
                copy.wait_send()
            for side in range(2):
                rim_ans[side, 1] = jnp.where(inside[side], rims[side, :, 0], 0.0)
                rim_base[side] = jnp.where(inside[side], rims[side, :, 1], 0.0)

        rim_p = [rim_ans[side, 1] for side in range(2)]
        rim_m = [mobility(rim_base[side], rim_p[side]) for side in range(2)]
        first_p, first_m = x[:, 0, 0], mob[0]
        last_p, last_m = x[:, 0, tiles - 1], mob[tiles - 1]
        p_was = jnp.where(sub == 0, rim_p[0], later(last_p, 1))
        m_was = jnp.where(sub == 0, rim_m[0], later(last_m, 1))
        p, m = first_p, first_m
        flux = 0.5 * (m + m_was) * (p - p_was)
        for t in range(tiles):
            if t + 1 < tiles:
                p_next, m_next = x[:, 0, t + 1], mob[t + 1]
            else:
                p_next = jnp.where(sub == SUB - 1, rim_p[1], sooner(first_p, 1))
                m_next = jnp.where(sub == SUB - 1, rim_m[1], sooner(first_m, 1))
            flux_next = 0.5 * (m_next + m) * (p_next - p)
            along = 0.5 * (m + left(m)) * (p - left(p))
            p_wide = jnp.concatenate([none, p, none], axis=0)
            m_wide = jnp.concatenate([none, m, none], axis=0)
            over = 0.5 * (m_wide[1:] + m_wide[:-1]) * (p_wide[1:] - p_wide[:-1])
            applied = STORE * p + (flux - flux_next) + (along - right(along)) + (over[:-1] - over[1:])
            res[:, t] = jnp.where(valid, x[:, 2, t] - applied, 0.0)
            ans[t] = jnp.zeros_like(p)
            p, m, flux = p_next, m_next, flux_next
            if t == tiles // 2 - 1:
                finish()
                total = near_box[parity, 0, 0]
                for a in range(1, members):
                    total = total + near_box[parity, a, 0]
                far_box[parity, group] = total
                finish = trade_far(total, total, parity)

        @pl.when(step == DEFECT - 1)
        def _():
            for copy in finals(1):
                copy.start()

        finish()
        total = far_box[parity, 0]
        for a in range(1, groups):
            total = total + far_box[parity, a]
        mref = total * (1.0 / dips)

        root = jnp.sqrt((STORE + 4.0 * mref) * (STORE + 8.0 * mref))
        q = 2.0 * mref / (STORE + 6.0 * mref + root)
        gain = 1.0 / root
        chunk = power(q, tiles)
        block = power(q, rows)
        cluster = power(block, members)
        whole = power(cluster, groups)
        unmirror = 1.0 / (1.0 - whole * whole)
        mirror_up = jnp.ones_like(q)
        mirror_down = mirror_up
        twice = cluster * cluster
        for a in range(groups - 1):
            mirror_up = jnp.where(a < group, mirror_up * twice, mirror_up)
            mirror_down = jnp.where(a < groups - 1 - group, mirror_down * twice, mirror_down)
        for i, value in enumerate((chunk, block, cluster, unmirror, mirror_up, mirror_down)):
            col[i] = value
        spread = (crosses, SUB, width)
        for i, value in enumerate((mref, q, gain)):
            full[i] = jnp.broadcast_to(value, spread)
        running = q
        for t in range(tiles):
            qpow[t] = jnp.broadcast_to(running, spread)
            running = running * q
        ahead = jnp.ones((crosses, SUB, width), jnp.float32)
        behind = ahead
        step_up = jnp.broadcast_to(chunk, ahead.shape)
        for bit in (1, 2, 4):
            ahead = jnp.where((sub & bit) != 0, ahead * step_up, ahead)
            behind = jnp.where((sub & bit) == 0, behind * step_up, behind)
            step_up = step_up * step_up
        part[0], part[1] = ahead, behind
        for side in range(2):
            rim_ans[side, 0] = jnp.zeros((crosses, 1, width), jnp.float32)

        def sweep(j, carry):
            parity = lax.rem(turn + 1 + j, 2)
            weight = jnp.float32(omega[0])
            for i in range(1, SWEEPS):
                weight = jnp.where(j == i, jnp.float32(omega[i]), weight)
            keep = 1.0 - weight
            mref, q, chunk = full[0], full[1], col[0]

            y = jnp.zeros((crosses, SUB, width), jnp.float32)
            for t in range(tiles):
                u = ans[t]
                near = left(u) + right(u)
                if crosses > 1:
                    near = near + jnp.concatenate([none, u[:-1]], axis=0)
                    near = near + jnp.concatenate([u[1:], none], axis=0)
                r = res[:, t] + mref * near
                mob[t] = r
                y = r + q * y
                qv = y - r
                part[2 + t] = qv
            z = jnp.zeros((crosses, SUB, width), jnp.float32)
            for t in reversed(range(tiles)):
                z = mob[t] + q * z
                part[2 + t] = part[2 + t] + z
            step_up = chunk
            for k in (1, 2, 4):
                y = y + step_up * jnp.where(sub >= k, later(y, k), 0.0)
                z = z + step_up * jnp.where(sub < SUB - k, sooner(z, k), 0.0)
                step_up = step_up * step_up
            tail, head = y[:, SUB - 1 :, :], z[:, :1, :]
            trade_near([tail, head], parity)()

            block, cluster, unmirror = col[1], col[2], col[3]
            fore = near_box[parity, 0, 0]
            back = near_box[parity, members - 1, 1]
            for a in range(1, members):
                fore = fore * block + near_box[parity, a, 0]
                back = back * block + near_box[parity, members - 1 - a, 1]
            mirror_up, mirror_down = col[4], col[5]
            upward = fore + mirror_up * cluster * back
            downward = back + mirror_down * cluster * fore
            trade_far(upward, downward, parity)()
            from_left = jnp.zeros_like(upward)
            from_right = jnp.zeros_like(upward)
            for a in range(groups - 1):
                b = groups - 1 - a
                from_left = jnp.where(
                    a < group, from_left * cluster + far_box[parity, a], from_left
                )
                from_right = jnp.where(
                    b > group, from_right * cluster + far_box[parity, b], from_right
                )
            from_left, from_right = (
                (from_left + mirror_up * (from_right * cluster + downward)) * unmirror,
                (from_right + mirror_down * (from_left * cluster + upward)) * unmirror,
            )
            for a in range(members - 1):
                b = members - 1 - a
                from_left = jnp.where(
                    a < member, from_left * block + near_box[parity, a, 0], from_left
                )
                from_right = jnp.where(
                    b > member, from_right * block + near_box[parity, b, 1], from_right
                )

            thin_q = q[:, :1, :]
            scale = weight * full[2]
            thin_scale = scale[:, :1, :]
            rim_ans[0, 0] = keep * rim_ans[0, 0] + thin_scale * (
                from_left + thin_q * (head + block * from_right)
            )
            rim_ans[1, 0] = keep * rim_ans[1, 0] + thin_scale * (
                from_right + thin_q * (tail + block * from_left)
            )
            y = jnp.where(sub >= 1, later(y, 1), 0.0) + part[0] * from_left
            z = jnp.where(sub < SUB - 1, sooner(z, 1), 0.0) + part[1] * from_right
            for t in range(tiles):
                solved = part[2 + t] + qpow[t] * y + qpow[tiles - 1 - t] * z
                ans[t] = keep * ans[t] + scale * solved
            return carry

        lax.fori_loop(0, SWEEPS, sweep, 0)
        for t in range(tiles):
            x[:, 0, t] = x[:, 0, t] + ans[t]
        for side in range(2):
            rim_ans[side, 1] = rim_ans[side, 1] + jnp.where(inside[side], rim_ans[side, 0], 0.0)
        return carry

    lax.fori_loop(0, DEFECT, one_step, 0)

    for copy in finals(0):
        copy.start()
    for which in (1, 0):
        ref = out_p if which == 0 else out_d
        for k in range(crosses):
            to, frm = across(k), before(k)
            arrived(
                ref.at[:, :, 0, columns(frm * main, main)], out_sems, (which, k), (to, strike), k
            )
    for k in range(1, crosses):
        to = across(k)
        for f in range(3):
            body, edge = landing(f, cross)
            send(body, body, cross_sems, (f, k), (to, strike), k).wait_send()
            send(edge, edge, halo_sems, (f, k), (to, strike), k).wait_send()
        for which in range(2):
            src = x.at[to, 0] if which == 0 else res.at[to]
            src = src.at[:, :, pl.ds(0, main)]
            send(src, src, out_sems, (which, k), (to, strike), k).wait_send()


def per_device(pressure, source, facies, mobility_table):
    crosses = lax.axis_size("cross")
    strikes = lax.axis_size("strike")
    rows, _, cells = pressure.shape
    tiles = rows // SUB
    main = cells // crosses
    width = main + LANES
    members = 1
    groups = strikes // members

    def dealt(a):
        return a.reshape(SUB, tiles, 1, cells)

    f32 = jnp.float32
    vm = pltpu.VMEM
    dma = pltpu.SemaphoreType.DMA
    full = (crosses, SUB, width)
    field = (tiles,) + full
    thin = (crosses, 1, width)
    whole = jax.ShapeDtypeStruct((SUB, tiles, 1, cells), f32)
    anywhere = pl.BlockSpec(memory_space=pltpu.HBM)
    outs = pl.pallas_call(
        functools.partial(kernel, crosses, strikes, rows * strikes),
        out_shape=[whole, whole],
        in_specs=[anywhere] * 3 + [pl.BlockSpec(memory_space=pltpu.SMEM)],
        out_specs=[anywhere] * 2,
        scratch_shapes=[
            vm((crosses, 3, tiles, SUB, width), f32),
            vm((crosses, tiles, SUB, width), jnp.int32),
            vm((crosses, 2, 2, tiles, SUB, LANES), f32),
            vm((crosses, 2, tiles, SUB, LANES), jnp.int32),
            vm((2, crosses, 2, 1, width), f32),
            vm(field, f32),
            vm((crosses, tiles, SUB, width), f32),
            vm(field, f32),
            vm((tiles + 2,) + full, f32),
            vm(field, f32),
            vm((3,) + full, f32),
            vm((6,) + thin, f32),
            vm((2, 2) + thin, f32),
            vm((2,) + thin, f32),
            vm((2, members, 2) + thin, f32),
            vm((2, groups) + thin, f32),
            vm((2, 2) + thin, f32),
            dma((2, 3, crosses)),
            dma((2, 3, crosses)),
            dma((2, 2)),
            dma((2, 2, max(members - 1, 1))),
            dma((2, 2, max(groups - 1, 1))),
            dma((2, 2, crosses)),
        ],
        compiler_params=pltpu.CompilerParams(
            collective_id=0, has_side_effects=True, vmem_limit_bytes=40 * 1024 * 1024
        ),
    )(dealt(pressure), dealt(facies), dealt(source), mobility_table)
    return tuple(a.reshape(rows, 1, cells) for a in outs)


def solution(mesh):
    in_specs = (
        P("strike", "cross", None),
        P("strike", "cross", None),
        P("strike", "cross", None),
        P(),
    )
    out_specs = (P("strike", "cross", None), P("strike", "cross", None))
    return jax.shard_map(
        per_device, mesh=mesh, in_specs=in_specs, out_specs=out_specs, check_vma=False
    )
```

```python
import functools
import math

import jax
import jax.numpy as jnp
from jax import lax
from jax.experimental import pallas as pl
from jax.experimental.pallas import tpu as pltpu
from jax.sharding import PartitionSpec as P

CLASSES = 8
DEFECT = 2
SWEEPS = 3

STORE = 0.5
LOW = 0.05
HIGH = 1.95

SUB = 8
LANES = 128
HALF = LANES // 2
MESH = pl.DeviceIdType.MESH


def chebyshev_weights(count):
    middle = 0.5 * (LOW + HIGH)
    half = 0.5 * (HIGH - LOW)
    return [
        1.0 / (middle + half * math.cos(math.pi * (2 * j + 1) / (2 * count))) for j in range(count)
    ]


def power(x, count):
    result = None
    while count:
        if count & 1:
            result = x if result is None else result * x
        count >>= 1
        if count:
            x = x * x
    return result


def kernel(
    crosses, strikes, dips, pressure, facies, source, table, out_p, out_d, x, fac, halo, halo_fac,
    rims, mob, res, ans, part, qpow, full, col, rim_ans, rim_base, far_box, far_out,
    cross_sems, halo_sems, rim_sems, far_sems, out_sems,
):
    tiles, width = x.shape[2], x.shape[4]
    main = width - LANES
    rows = tiles * SUB
    pieces = 2 if crosses % 2 == 0 else 1
    piece = crosses // pieces
    cross = lax.axis_index("cross")
    strike = lax.axis_index("strike")

    def across(k):
        return lax.rem(cross + k, crosses)

    def before(k):
        return lax.rem(cross + crosses - k, crosses)

    up = lax.rem(strike + 1, strikes)
    down = lax.rem(strike + strikes - 1, strikes)

    def peer_of(k):
        return (cross, lax.rem(strike + k, strikes))

    barrier = pltpu.get_barrier_semaphore()
    peers = [(across(k), strike) for k in range(1, crosses)]
    peers += [(cross, up), (cross, down)]
    peers += [peer_of(k) for k in range(1, strikes)]
    for peer in peers:
        pl.semaphore_signal(barrier, inc=1, device_id=peer, device_id_type=MESH)
    pl.semaphore_wait(barrier, len(peers))

    def send(src, dst, sems, where, target, k):
        if k == 0:
            return pltpu.make_async_copy(src, dst, sems.at[(1,) + where])
        return pltpu.make_async_remote_copy(
            src_ref=src,
            dst_ref=dst,
            send_sem=sems.at[(0,) + where],
            recv_sem=sems.at[(1,) + where],
            device_id=target,
            device_id_type=MESH,
        )

    def arrived(ref, sems, where, target, k):
        copy = send(ref, ref, sems, where, target, k)
        if k == 0:
            copy.wait()
        else:
            copy.wait_recv()

    def landing(f, c):
        if f == 1:
            return fac.at[c, :, :, pl.ds(0, main)], halo_fac.at[c]
        return x.at[c, f, :, :, pl.ds(0, main)], halo.at[c, f // 2]

    def columns(start, size):
        return pl.ds(pl.multiple_of(start, LANES), size)

    raws = (pressure, facies, source)
    for k in range(crosses):
        to = across(k)
        after = lax.rem(to + 1, crosses) * main
        ahead = lax.rem(to + crosses - 1, crosses) * main + main - LANES
        for f in range(3):
            body, edge = landing(f, cross)
            for t in range(tiles):
                send(
                    raws[f].at[:, t, 0, columns(to * main, main)], body.at[t],
                    cross_sems, (f, k), (to, strike), k,
                ).start()
            for t in range(tiles):
                for side, begin in ((0, after), (1, ahead)):
                    send(
                        raws[f].at[:, t, 0, columns(begin, LANES)], edge.at[side, t],
                        halo_sems, (f, k), (to, strike), k,
                    ).start()
    for k in range(crosses):
        for f in range(3):
            body, edge = landing(f, before(k))
            arrived(body, cross_sems, (f, k), (across(k), strike), k)
            arrived(edge, halo_sems, (f, k), (across(k), strike), k)

    inside = (strike > 0, strike < strikes - 1)
    lane = lax.broadcasted_iota(jnp.int32, (1, 1, width), 2)
    valid = (
        (lane < main)
        | ((lane < main + HALF) & (cross < crosses - 1))
        | ((lane >= main + HALF) & (cross > 0))
    )
    sub = lax.broadcasted_iota(jnp.int32, (1, SUB, width), 1)
    none = jnp.zeros((1, SUB, width), jnp.float32)
    tip = lax.broadcasted_iota(jnp.int32, (crosses, SUB, LANES), 2) < HALF
    real = valid[:, :, main:]

    def classed(codes):
        base = jnp.zeros(codes.shape, jnp.float32)
        for code in range(CLASSES):
            base = jnp.where(codes == code, table[code], base)
        return base

    for t in range(tiles):
        for f in (0, 2):
            merged = jnp.where(tip, halo[:, f // 2, 0, t], halo[:, f // 2, 1, t])
            x[:, f, t, :, main:] = jnp.where(real, merged, 0.0)
        merged = classed(jnp.where(tip, halo_fac[:, 0, t], halo_fac[:, 1, t]))
        x[:, 1, t, :, main:] = jnp.where(real, merged, 0.0)
        x[:, 1, t, :, :main] = classed(fac[:, t, :, :main])

    rim_copies = [
        send(
            x.at[:, pl.ds(0, 2), tile, pl.ds(row, 1), :], rims.at[side],
            rim_sems, (side,), (cross, target), 1,
        )
        for side, target, tile, row in ((0, up, tiles - 1, SUB - 1), (1, down, 0, 0))
    ]
    for copy in rim_copies:
        copy.start()

    def finals(which):
        ref = out_p if which == 0 else out_d
        copies = []
        for k in range(crosses):
            to = across(k)
            for t in range(tiles):
                src = x.at[to, 0, t] if which == 0 else res.at[to, t]
                copies.append(
                    send(
                        src.at[:, pl.ds(0, main)],
                        ref.at[:, t, 0, columns(cross * main, main)],
                        out_sems, (which, k), (to, strike), k,
                    )
                )
        return copies

    def left(a):
        return pltpu.roll(a, 1, 2)

    def right(a):
        return pltpu.roll(a, width - 1, 2)

    def later(a, k):
        return pltpu.roll(a, k, 1)

    def sooner(a, k):
        return pltpu.roll(a, SUB - k, 1)

    def mobility(base, p):
        return base * (1.0 + 0.5 * jnp.tanh(p))

    def trade(parity, which, low, size):
        def box(a):
            return far_box.at[parity, a, pl.ds(low, size)]

        copies = []
        for k in range(1, strikes):
            row = far_out.at[parity, lax.div(strike + k, strikes), pl.ds(low, size)]
            copy = send(row, box(strike), far_sems, (parity, which, k - 1), peer_of(k), k)
            copy.start()
            copies.append(copy)

        def finish():
            for k in range(1, strikes):
                origin = lax.rem(strike + strikes - k, strikes)
                arrived(box(origin), far_sems, (parity, which, k - 1), peer_of(k), k)

        def settle():
            for copy in copies:
                copy.wait_send()

        return finish, settle

    omega = chebyshev_weights(SWEEPS)

    def one_step(step, carry):
        turn = step * (SWEEPS + 1)
        parity = lax.rem(turn, 2)
        total = jnp.zeros((crosses, SUB, width), jnp.float32)
        for t in range(tiles):
            m = mobility(x[:, 1, t], x[:, 0, t])
            mob[t] = m
            total = total + m
        total = jnp.sum(total, axis=1, keepdims=True)
        far_out[parity, 0] = total
        far_out[parity, 1] = total
        far_box[parity, strike] = total
        finish, settle = trade(parity, 0, 0, crosses)

        @pl.when(step == 0)
        def _():
            for copy in rim_copies:
                copy.wait_recv()
            for copy in rim_copies:
                copy.wait_send()
            for side in range(2):
                rim_ans[side, 1] = jnp.where(inside[side], rims[side, :, 0], 0.0)
                rim_base[side] = jnp.where(inside[side], rims[side, :, 1], 0.0)

        rim_p = [rim_ans[side, 1] for side in range(2)]
        rim_m = [mobility(rim_base[side], rim_p[side]) for side in range(2)]
        first_p, first_m = x[:, 0, 0], mob[0]
        last_p, last_m = x[:, 0, tiles - 1], mob[tiles - 1]
        p_was = jnp.where(sub == 0, rim_p[0], later(last_p, 1))
        m_was = jnp.where(sub == 0, rim_m[0], later(last_m, 1))
        p, m = first_p, first_m
        flux = 0.5 * (m + m_was) * (p - p_was)
        for t in range(tiles):
            if t + 1 < tiles:
                p_next, m_next = x[:, 0, t + 1], mob[t + 1]
            else:
                p_next = jnp.where(sub == SUB - 1, rim_p[1], sooner(first_p, 1))
                m_next = jnp.where(sub == SUB - 1, rim_m[1], sooner(first_m, 1))
            flux_next = 0.5 * (m_next + m) * (p_next - p)
            along = 0.5 * (m + left(m)) * (p - left(p))
            p_wide = jnp.concatenate([none, p, none], axis=0)
            m_wide = jnp.concatenate([none, m, none], axis=0)
            over = 0.5 * (m_wide[1:] + m_wide[:-1]) * (p_wide[1:] - p_wide[:-1])
            applied = STORE * p + (flux - flux_next) + (along - right(along)) + (over[:-1] - over[1:])
            res[:, t] = jnp.where(valid, x[:, 2, t] - applied, 0.0)
            ans[t] = jnp.zeros_like(p)
            p, m, flux = p_next, m_next, flux_next

        @pl.when(step == DEFECT - 1)
        def _():
            for copy in finals(1):
                copy.start()

        finish()
        settle()
        total = far_box[parity, 0]
        for a in range(1, strikes):
            total = total + far_box[parity, a]
        mref = total * (1.0 / dips)

        root = jnp.sqrt((STORE + 4.0 * mref) * (STORE + 8.0 * mref))
        q = 2.0 * mref / (STORE + 6.0 * mref + root)
        gain = 1.0 / root
        chunk = power(q, tiles)
        block = power(q, rows)
        whole = power(block, strikes)
        unmirror = 1.0 / (1.0 - whole * whole)
        mirror_up = jnp.ones_like(q)
        mirror_down = mirror_up
        twice = block * block
        for a in range(strikes - 1):
            mirror_up = jnp.where(a < strike, mirror_up * twice, mirror_up)
            mirror_down = jnp.where(a < strikes - 1 - strike, mirror_down * twice, mirror_down)
        for i, value in enumerate((chunk, block, unmirror, mirror_up, mirror_down)):
            col[i] = value
        spread = (crosses, SUB, width)
        for i, value in enumerate((mref, q, gain)):
            full[i] = jnp.broadcast_to(value, spread)
        running = q
        for t in range(tiles):
            qpow[t] = jnp.broadcast_to(running, spread)
            running = running * q
        ahead = jnp.ones((crosses, SUB, width), jnp.float32)
        behind = ahead
        step_up = jnp.broadcast_to(chunk, ahead.shape)
        for bit in (1, 2, 4):
            ahead = jnp.where((sub & bit) != 0, ahead * step_up, ahead)
            behind = jnp.where((sub & bit) == 0, behind * step_up, behind)
            step_up = step_up * step_up
        part[0], part[1] = ahead, behind
        for side in range(2):
            rim_ans[side, 0] = jnp.zeros((crosses, 1, width), jnp.float32)

        def sweep(j, carry):
            parity = lax.rem(turn + 1 + j, 2)
            weight = jnp.float32(omega[0])
            for i in range(1, SWEEPS):
                weight = jnp.where(j == i, jnp.float32(omega[i]), weight)
            keep = 1.0 - weight
            waiting = []
            for which in range(pieces):
                low, high = which * piece, (which + 1) * piece
                mref, q, chunk = full[0, low:high], full[1, low:high], col[0, low:high]
                y = jnp.zeros((piece, SUB, width), jnp.float32)
                for t in range(tiles):
                    u = ans[t, low:high]
                    near = left(u) + right(u)
                    if low > 0:
                        near = near + ans[t, low - 1 : high - 1]
                    elif piece > 1:
                        near = near + jnp.concatenate([none, u[:-1]], axis=0)
                    if high < crosses:
                        near = near + ans[t, low + 1 : high + 1]
                    elif piece > 1:
                        near = near + jnp.concatenate([u[1:], none], axis=0)
                    r = res[low:high, t] + mref * near
                    mob[t, low:high] = r
                    y = q * y
                    part[2 + t, low:high] = y
                    y = r + y
                z = jnp.zeros((piece, SUB, width), jnp.float32)
                for t in reversed(range(tiles)):
                    z = mob[t, low:high] + q * z
                    part[2 + t, low:high] = part[2 + t, low:high] + z
                step_up = chunk
                for k in (1, 2, 4):
                    y = y + step_up * jnp.where(sub >= k, later(y, k), 0.0)
                    z = z + step_up * jnp.where(sub < SUB - k, sooner(z, k), 0.0)
                    step_up = step_up * step_up
                tail, head = y[:, SUB - 1 :, :], z[:, :1, :]
                block = col[1, low:high]
                far_out[parity, 0, low:high] = tail + col[3, low:high] * block * head
                far_out[parity, 1, low:high] = head + col[4, low:high] * block * tail
                waiting.append((y, z, tail, head) + trade(parity, which, low, piece))

            for which in range(pieces):
                low, high = which * piece, (which + 1) * piece
                y, z, tail, head, finish, settle = waiting[which]
                block, unmirror = col[1, low:high], col[2, low:high]
                mirror_up, mirror_down = col[3, low:high], col[4, low:high]
                thin_q = full[1, low:high, :1, :]
                scale = weight * full[2, low:high]
                thin_scale = weight * full[2, low:high, :1, :]
                upward = far_out[parity, 0, low:high]
                downward = far_out[parity, 1, low:high]
                finish()
                from_left = jnp.zeros_like(upward)
                from_right = jnp.zeros_like(upward)
                for a in range(strikes - 1):
                    b = strikes - 1 - a
                    from_left = jnp.where(
                        a < strike, from_left * block + far_box[parity, a, low:high], from_left
                    )
                    from_right = jnp.where(
                        b > strike, from_right * block + far_box[parity, b, low:high], from_right
                    )
                from_left, from_right = (
                    (from_left + mirror_up * (from_right * block + downward)) * unmirror,
                    (from_right + mirror_down * (from_left * block + upward)) * unmirror,
                )
                rim_ans[0, 0, low:high] = keep * rim_ans[0, 0, low:high] + thin_scale * (
                    from_left + thin_q * (head + block * from_right)
                )
                rim_ans[1, 0, low:high] = keep * rim_ans[1, 0, low:high] + thin_scale * (
                    from_right + thin_q * (tail + block * from_left)
                )
                y = jnp.where(sub >= 1, later(y, 1), 0.0) + part[0, low:high] * from_left
                z = jnp.where(sub < SUB - 1, sooner(z, 1), 0.0) + part[1, low:high] * from_right
                for t in range(tiles):
                    solved = part[2 + t, low:high] + (
                        qpow[t, low:high] * y + qpow[tiles - 1 - t, low:high] * z
                    )
                    ans[t, low:high] = keep * ans[t, low:high] + scale * solved
            for which in range(pieces):
                waiting[which][5]()
            return carry

        lax.fori_loop(0, SWEEPS, sweep, 0)
        for t in range(tiles):
            x[:, 0, t] = x[:, 0, t] + ans[t]
        for side in range(2):
            rim_ans[side, 1] = rim_ans[side, 1] + jnp.where(inside[side], rim_ans[side, 0], 0.0)
        return carry

    lax.fori_loop(0, DEFECT, one_step, 0)

    for copy in finals(0):
        copy.start()
    for which in (1, 0):
        ref = out_p if which == 0 else out_d
        for k in range(crosses):
            to, frm = across(k), before(k)
            arrived(
                ref.at[:, :, 0, columns(frm * main, main)], out_sems, (which, k), (to, strike), k
            )
    for k in range(1, crosses):
        to = across(k)
        for f in range(3):
            body, edge = landing(f, cross)
            send(body, body, cross_sems, (f, k), (to, strike), k).wait_send()
            send(edge, edge, halo_sems, (f, k), (to, strike), k).wait_send()
        for which in range(2):
            src = x.at[to, 0] if which == 0 else res.at[to]
            src = src.at[:, :, pl.ds(0, main)]
            send(src, src, out_sems, (which, k), (to, strike), k).wait_send()


def per_device(pressure, source, facies, mobility_table):
    crosses = lax.axis_size("cross")
    strikes = lax.axis_size("strike")
    rows, _, cells = pressure.shape
    tiles = rows // SUB
    main = cells // crosses
    width = main + LANES

    def dealt(a):
        return a.reshape(SUB, tiles, 1, cells)

    f32 = jnp.float32
    vm = pltpu.VMEM
    dma = pltpu.SemaphoreType.DMA
    full = (crosses, SUB, width)
    field = (tiles,) + full
    thin = (crosses, 1, width)
    whole = jax.ShapeDtypeStruct((SUB, tiles, 1, cells), f32)
    anywhere = pl.BlockSpec(memory_space=pltpu.HBM)
    outs = pl.pallas_call(
        functools.partial(kernel, crosses, strikes, rows * strikes),
        out_shape=[whole, whole],
        in_specs=[anywhere] * 3 + [pl.BlockSpec(memory_space=pltpu.SMEM)],
        out_specs=[anywhere] * 2,
        scratch_shapes=[
            vm((crosses, 3, tiles, SUB, width), f32),
            vm((crosses, tiles, SUB, width), jnp.int32),
            vm((crosses, 2, 2, tiles, SUB, LANES), f32),
            vm((crosses, 2, tiles, SUB, LANES), jnp.int32),
            vm((2, crosses, 2, 1, width), f32),
            vm(field, f32),
            vm((crosses, tiles, SUB, width), f32),
            vm(field, f32),
            vm((tiles + 2,) + full, f32),
            vm(field, f32),
            vm((3,) + full, f32),
            vm((5,) + thin, f32),
            vm((2, 2) + thin, f32),
            vm((2,) + thin, f32),
            vm((2, strikes) + thin, f32),
            vm((2, 2) + thin, f32),
            dma((2, 3, crosses)),
            dma((2, 3, crosses)),
            dma((2, 2)),
            dma((2, 2, 2, max(strikes - 1, 1))),
            dma((2, 2, crosses)),
        ],
        compiler_params=pltpu.CompilerParams(
            collective_id=0, has_side_effects=True, vmem_limit_bytes=60 * 1024 * 1024
        ),
    )(dealt(pressure), dealt(facies), dealt(source), mobility_table)
    return tuple(a.reshape(rows, 1, cells) for a in outs)


def solution(mesh):
    in_specs = (
        P("strike", "cross", None),
        P("strike", "cross", None),
        P("strike", "cross", None),
        P(),
    )
    out_specs = (P("strike", "cross", None), P("strike", "cross", None))
    return jax.shard_map(
        per_device, mesh=mesh, in_specs=in_specs, out_specs=out_specs, check_vma=False
    )
```

```python
import functools
import math

import jax
import jax.numpy as jnp
from jax import lax
from jax.experimental import pallas as pl
from jax.experimental.pallas import tpu as pltpu
from jax.sharding import PartitionSpec as P

CLASSES = 8
DEFECT = 2
SWEEPS = 3

STORE = 0.5
LOW = 0.05
HIGH = 1.95

SUB = 8
LANES = 128
HALF = LANES // 2
MESH = pl.DeviceIdType.MESH


def chebyshev_weights(count):
    middle = 0.5 * (LOW + HIGH)
    half = 0.5 * (HIGH - LOW)
    return [
        1.0 / (middle + half * math.cos(math.pi * (2 * j + 1) / (2 * count))) for j in range(count)
    ]


def power(x, count):
    result = None
    while count:
        if count & 1:
            result = x if result is None else result * x
        count >>= 1
        if count:
            x = x * x
    return result


def kernel(
    crosses, strikes, dips, pressure, facies, source, table, out_p, out_d, x, fac, halo, halo_fac,
    rims, mob, res, ans, part, qpow, full, col, rim_ans, rim_base, far_box, far_out,
    cross_sems, halo_sems, rim_sems, far_sems, out_sems,
):
    tiles, width = x.shape[2], x.shape[4]
    main = width - LANES
    rows = tiles * SUB
    pieces = 2 if crosses % 2 == 0 else 1
    piece = crosses // pieces
    cross = lax.axis_index("cross")
    strike = lax.axis_index("strike")

    def across(k):
        return lax.rem(cross + k, crosses)

    def before(k):
        return lax.rem(cross + crosses - k, crosses)

    up = lax.rem(strike + 1, strikes)
    down = lax.rem(strike + strikes - 1, strikes)

    def peer_of(k):
        return (cross, lax.rem(strike + k, strikes))

    barrier = pltpu.get_barrier_semaphore()
    peers = [(across(k), strike) for k in range(1, crosses)]
    peers += [(cross, up), (cross, down)]
    peers += [peer_of(k) for k in range(1, strikes)]
    for peer in peers:
        pl.semaphore_signal(barrier, inc=1, device_id=peer, device_id_type=MESH)

    def send(src, dst, sems, where, target, k):
        if k == 0:
            return pltpu.make_async_copy(src, dst, sems.at[(1,) + where])
        return pltpu.make_async_remote_copy(
            src_ref=src,
            dst_ref=dst,
            send_sem=sems.at[(0,) + where],
            recv_sem=sems.at[(1,) + where],
            device_id=target,
            device_id_type=MESH,
        )

    def arrived(ref, sems, where, target, k):
        copy = send(ref, ref, sems, where, target, k)
        if k == 0:
            copy.wait()
        else:
            copy.wait_recv()

    def landing(f, c):
        if f == 1:
            return fac.at[c, :, :, pl.ds(0, main)], halo_fac.at[c]
        return x.at[c, f, :, :, pl.ds(0, main)], halo.at[c, f // 2]

    def columns(start, size):
        return pl.ds(pl.multiple_of(start, LANES), size)

    raws = (pressure, facies, source)

    def deal(k):
        to = across(k)
        after = lax.rem(to + 1, crosses) * main
        ahead = lax.rem(to + crosses - 1, crosses) * main + main - LANES
        for f in range(3):
            body, edge = landing(f, cross)
            for t in range(tiles):
                send(
                    raws[f].at[:, t, 0, columns(to * main, main)], body.at[t],
                    cross_sems, (f, k), (to, strike), k,
                ).start()
            for t in range(tiles):
                for side, begin in ((0, after), (1, ahead)):
                    send(
                        raws[f].at[:, t, 0, columns(begin, LANES)], edge.at[side, t],
                        halo_sems, (f, k), (to, strike), k,
                    ).start()

    def dealt(f):
        for k in range(crosses):
            body, edge = landing(f, before(k))
            arrived(body, cross_sems, (f, k), (across(k), strike), k)
            arrived(edge, halo_sems, (f, k), (across(k), strike), k)

    deal(0)
    pl.semaphore_wait(barrier, len(peers))
    for k in range(1, crosses):
        deal(k)
    dealt(0)
    dealt(1)

    inside = (strike > 0, strike < strikes - 1)
    lane = lax.broadcasted_iota(jnp.int32, (1, 1, width), 2)
    valid = (
        (lane < main)
        | ((lane < main + HALF) & (cross < crosses - 1))
        | ((lane >= main + HALF) & (cross > 0))
    )
    sub = lax.broadcasted_iota(jnp.int32, (1, SUB, width), 1)
    none = jnp.zeros((1, SUB, width), jnp.float32)
    tip = lax.broadcasted_iota(jnp.int32, (crosses, SUB, LANES), 2) < HALF
    real = valid[:, :, main:]

    def classed(codes):
        base = jnp.zeros(codes.shape, jnp.float32)
        for code in range(CLASSES):
            base = jnp.where(codes == code, table[code], base)
        return base

    def joined(f):
        for t in range(tiles):
            merged = jnp.where(tip, halo[:, f // 2, 0, t], halo[:, f // 2, 1, t])
            x[:, f, t, :, main:] = jnp.where(real, merged, 0.0)

    joined(0)
    for t in range(tiles):
        merged = classed(jnp.where(tip, halo_fac[:, 0, t], halo_fac[:, 1, t]))
        x[:, 1, t, :, main:] = jnp.where(real, merged, 0.0)
        x[:, 1, t, :, :main] = classed(fac[:, t, :, :main])

    rim_copies = [
        send(
            x.at[:, pl.ds(0, 2), tile, pl.ds(row, 1), :], rims.at[side],
            rim_sems, (side,), (cross, target), 1,
        )
        for side, target, tile, row in ((0, up, tiles - 1, SUB - 1), (1, down, 0, 0))
    ]
    for copy in rim_copies:
        copy.start()

    def finals(which):
        ref = out_p if which == 0 else out_d
        copies = []
        for k in range(crosses):
            to = across(k)
            for t in range(tiles):
                src = x.at[to, 0, t] if which == 0 else res.at[to, t]
                copies.append(
                    send(
                        src.at[:, pl.ds(0, main)],
                        ref.at[:, t, 0, columns(cross * main, main)],
                        out_sems, (which, k), (to, strike), k,
                    )
                )
        return copies

    def left(a):
        return pltpu.roll(a, 1, 2)

    def right(a):
        return pltpu.roll(a, width - 1, 2)

    def later(a, k):
        return pltpu.roll(a, k, 1)

    def sooner(a, k):
        return pltpu.roll(a, SUB - k, 1)

    def mobility(base, p):
        return base * (1.0 + 0.5 * jnp.tanh(p))

    def trade(parity, which, low, size):
        def box(a):
            return far_box.at[parity, a, pl.ds(low, size)]

        copies = []
        for k in range(1, strikes):
            row = far_out.at[parity, lax.div(strike + k, strikes), pl.ds(low, size)]
            copy = send(row, box(strike), far_sems, (parity, which, k - 1), peer_of(k), k)
            copy.start()
            copies.append(copy)

        def finish():
            for k in range(1, strikes):
                origin = lax.rem(strike + strikes - k, strikes)
                arrived(box(origin), far_sems, (parity, which, k - 1), peer_of(k), k)

        def settle():
            for copy in copies:
                copy.wait_send()

        return finish, settle

    omega = chebyshev_weights(SWEEPS)

    def one_step(step, carry):
        turn = step * (SWEEPS + 1)
        parity = lax.rem(turn, 2)
        total = jnp.zeros((crosses, SUB, width), jnp.float32)
        for t in range(tiles):
            m = mobility(x[:, 1, t], x[:, 0, t])
            mob[t] = m
            total = total + m
        total = jnp.sum(total, axis=1, keepdims=True)
        far_out[parity, 0] = total
        far_out[parity, 1] = total
        far_box[parity, strike] = total
        finish, settle = trade(parity, 0, 0, crosses)

        @pl.when(step == 0)
        def _():
            for copy in rim_copies:
                copy.wait_recv()
            for copy in rim_copies:
                copy.wait_send()
            for side in range(2):
                rim_ans[side, 1] = jnp.where(inside[side], rims[side, :, 0], 0.0)
                rim_base[side] = jnp.where(inside[side], rims[side, :, 1], 0.0)
            dealt(2)
            joined(2)

        rim_p = [rim_ans[side, 1] for side in range(2)]
        rim_m = [mobility(rim_base[side], rim_p[side]) for side in range(2)]
        first_p, first_m = x[:, 0, 0], mob[0]
        last_p, last_m = x[:, 0, tiles - 1], mob[tiles - 1]
        p_was = jnp.where(sub == 0, rim_p[0], later(last_p, 1))
        m_was = jnp.where(sub == 0, rim_m[0], later(last_m, 1))
        p, m = first_p, first_m
        flux = 0.5 * (m + m_was) * (p - p_was)
        for t in range(tiles):
            if t + 1 < tiles:
                p_next, m_next = x[:, 0, t + 1], mob[t + 1]
            else:
                p_next = jnp.where(sub == SUB - 1, rim_p[1], sooner(first_p, 1))
                m_next = jnp.where(sub == SUB - 1, rim_m[1], sooner(first_m, 1))
            flux_next = 0.5 * (m_next + m) * (p_next - p)
            along = 0.5 * (m + left(m)) * (p - left(p))
            p_wide = jnp.concatenate([none, p, none], axis=0)
            m_wide = jnp.concatenate([none, m, none], axis=0)
            over = 0.5 * (m_wide[1:] + m_wide[:-1]) * (p_wide[1:] - p_wide[:-1])
            applied = STORE * p + (flux - flux_next) + (along - right(along)) + (over[:-1] - over[1:])
            res[:, t] = jnp.where(valid, x[:, 2, t] - applied, 0.0)
            ans[t] = jnp.zeros_like(p)
            p, m, flux = p_next, m_next, flux_next

        @pl.when(step == DEFECT - 1)
        def _():
            for copy in finals(1):
                copy.start()

        finish()
        settle()
        total = far_box[parity, 0]
        for a in range(1, strikes):
            total = total + far_box[parity, a]
        mref = total * (1.0 / dips)

        root = jnp.sqrt((STORE + 4.0 * mref) * (STORE + 8.0 * mref))
        q = 2.0 * mref / (STORE + 6.0 * mref + root)
        gain = 1.0 / root
        chunk = power(q, tiles)
        block = power(q, rows)
        whole = power(block, strikes)
        unmirror = 1.0 / (1.0 - whole * whole)
        mirror_up = jnp.ones_like(q)
        mirror_down = mirror_up
        twice = block * block
        for a in range(strikes - 1):
            mirror_up = jnp.where(a < strike, mirror_up * twice, mirror_up)
            mirror_down = jnp.where(a < strikes - 1 - strike, mirror_down * twice, mirror_down)
        for i, value in enumerate((chunk, block, unmirror, mirror_up, mirror_down)):
            col[i] = value
        spread = (crosses, SUB, width)
        for i, value in enumerate((mref, q, gain)):
            full[i] = jnp.broadcast_to(value, spread)
        running = q
        for t in range(tiles):
            qpow[t] = jnp.broadcast_to(running, spread)
            running = running * q
        ahead = jnp.ones((crosses, SUB, width), jnp.float32)
        behind = ahead
        step_up = jnp.broadcast_to(chunk, ahead.shape)
        for bit in (1, 2, 4):
            ahead = jnp.where((sub & bit) != 0, ahead * step_up, ahead)
            behind = jnp.where((sub & bit) == 0, behind * step_up, behind)
            step_up = step_up * step_up
        part[0], part[1] = ahead, behind
        for side in range(2):
            rim_ans[side, 0] = jnp.zeros((crosses, 1, width), jnp.float32)

        def sweep(j, carry):
            parity = lax.rem(turn + 1 + j, 2)
            weight = jnp.float32(omega[0])
            for i in range(1, SWEEPS):
                weight = jnp.where(j == i, jnp.float32(omega[i]), weight)
            keep = 1.0 - weight
            waiting = []
            for which in range(pieces):
                low, high = which * piece, (which + 1) * piece
                mref, q, chunk = full[0, low:high], full[1, low:high], col[0, low:high]
                y = jnp.zeros((piece, SUB, width), jnp.float32)
                for t in range(tiles):
                    u = ans[t, low:high]
                    near = left(u) + right(u)
                    if low > 0:
                        near = near + ans[t, low - 1 : high - 1]
                    elif piece > 1:
                        near = near + jnp.concatenate([none, u[:-1]], axis=0)
                    if high < crosses:
                        near = near + ans[t, low + 1 : high + 1]
                    elif piece > 1:
                        near = near + jnp.concatenate([u[1:], none], axis=0)
                    r = res[low:high, t] + mref * near
                    mob[t, low:high] = r
                    y = q * y
                    part[2 + t, low:high] = y
                    y = r + y
                z = jnp.zeros((piece, SUB, width), jnp.float32)
                for t in reversed(range(tiles)):
                    z = mob[t, low:high] + q * z
                    part[2 + t, low:high] = part[2 + t, low:high] + z
                step_up = chunk
                for k in (1, 2, 4):
                    y = y + step_up * jnp.where(sub >= k, later(y, k), 0.0)
                    z = z + step_up * jnp.where(sub < SUB - k, sooner(z, k), 0.0)
                    step_up = step_up * step_up
                tail, head = y[:, SUB - 1 :, :], z[:, :1, :]
                block = col[1, low:high]
                far_out[parity, 0, low:high] = tail + col[3, low:high] * block * head
                far_out[parity, 1, low:high] = head + col[4, low:high] * block * tail
                waiting.append((y, z, tail, head) + trade(parity, which, low, piece))

            for which in range(pieces):
                low, high = which * piece, (which + 1) * piece
                y, z, tail, head, finish, settle = waiting[which]
                block, unmirror = col[1, low:high], col[2, low:high]
                mirror_up, mirror_down = col[3, low:high], col[4, low:high]
                thin_q = full[1, low:high, :1, :]
                scale = weight * full[2, low:high]
                thin_scale = weight * full[2, low:high, :1, :]
                upward = far_out[parity, 0, low:high]
                downward = far_out[parity, 1, low:high]
                finish()
                from_left = jnp.zeros_like(upward)
                from_right = jnp.zeros_like(upward)
                for a in range(strikes - 1):
                    b = strikes - 1 - a
                    from_left = jnp.where(
                        a < strike, from_left * block + far_box[parity, a, low:high], from_left
                    )
                    from_right = jnp.where(
                        b > strike, from_right * block + far_box[parity, b, low:high], from_right
                    )
                from_left, from_right = (
                    (from_left + mirror_up * (from_right * block + downward)) * unmirror,
                    (from_right + mirror_down * (from_left * block + upward)) * unmirror,
                )
                rim_ans[0, 0, low:high] = keep * rim_ans[0, 0, low:high] + thin_scale * (
                    from_left + thin_q * (head + block * from_right)
                )
                rim_ans[1, 0, low:high] = keep * rim_ans[1, 0, low:high] + thin_scale * (
                    from_right + thin_q * (tail + block * from_left)
                )
                y = jnp.where(sub >= 1, later(y, 1), 0.0) + part[0, low:high] * from_left
                z = jnp.where(sub < SUB - 1, sooner(z, 1), 0.0) + part[1, low:high] * from_right
                for t in range(tiles):
                    solved = part[2 + t, low:high] + (
                        qpow[t, low:high] * y + qpow[tiles - 1 - t, low:high] * z
                    )
                    ans[t, low:high] = keep * ans[t, low:high] + scale * solved
            for which in range(pieces):
                waiting[which][5]()
            return carry

        lax.fori_loop(0, SWEEPS, sweep, 0)
        for t in range(tiles):
            x[:, 0, t] = x[:, 0, t] + ans[t]
        for side in range(2):
            rim_ans[side, 1] = rim_ans[side, 1] + jnp.where(inside[side], rim_ans[side, 0], 0.0)
        return carry

    lax.fori_loop(0, DEFECT, one_step, 0)

    for copy in finals(0):
        copy.start()
    for which in (1, 0):
        ref = out_p if which == 0 else out_d
        for k in range(crosses):
            to, frm = across(k), before(k)
            arrived(
                ref.at[:, :, 0, columns(frm * main, main)], out_sems, (which, k), (to, strike), k
            )
    for k in range(1, crosses):
        to = across(k)
        for f in range(3):
            body, edge = landing(f, cross)
            send(body, body, cross_sems, (f, k), (to, strike), k).wait_send()
            send(edge, edge, halo_sems, (f, k), (to, strike), k).wait_send()
        for which in range(2):
            src = x.at[to, 0] if which == 0 else res.at[to]
            src = src.at[:, :, pl.ds(0, main)]
            send(src, src, out_sems, (which, k), (to, strike), k).wait_send()


def per_device(pressure, source, facies, mobility_table):
    crosses = lax.axis_size("cross")
    strikes = lax.axis_size("strike")
    rows, _, cells = pressure.shape
    tiles = rows // SUB
    main = cells // crosses
    width = main + LANES

    def dealt(a):
        return a.reshape(SUB, tiles, 1, cells)

    f32 = jnp.float32
    vm = pltpu.VMEM
    dma = pltpu.SemaphoreType.DMA
    full = (crosses, SUB, width)
    field = (tiles,) + full
    thin = (crosses, 1, width)
    whole = jax.ShapeDtypeStruct((SUB, tiles, 1, cells), f32)
    anywhere = pl.BlockSpec(memory_space=pltpu.HBM)
    outs = pl.pallas_call(
        functools.partial(kernel, crosses, strikes, rows * strikes),
        out_shape=[whole, whole],
        in_specs=[anywhere] * 3 + [pl.BlockSpec(memory_space=pltpu.SMEM)],
        out_specs=[anywhere] * 2,
        scratch_shapes=[
            vm((crosses, 3, tiles, SUB, width), f32),
            vm((crosses, tiles, SUB, width), jnp.int32),
            vm((crosses, 2, 2, tiles, SUB, LANES), f32),
            vm((crosses, 2, tiles, SUB, LANES), jnp.int32),
            vm((2, crosses, 2, 1, width), f32),
            vm(field, f32),
            vm((crosses, tiles, SUB, width), f32),
            vm(field, f32),
            vm((tiles + 2,) + full, f32),
            vm(field, f32),
            vm((3,) + full, f32),
            vm((5,) + thin, f32),
            vm((2, 2) + thin, f32),
            vm((2,) + thin, f32),
            vm((2, strikes) + thin, f32),
            vm((2, 2) + thin, f32),
            dma((2, 3, crosses)),
            dma((2, 3, crosses)),
            dma((2, 2)),
            dma((2, 2, 2, max(strikes - 1, 1))),
            dma((2, 2, crosses)),
        ],
        compiler_params=pltpu.CompilerParams(
            collective_id=0, has_side_effects=True, vmem_limit_bytes=60 * 1024 * 1024
        ),
    )(dealt(pressure), dealt(facies), dealt(source), mobility_table)
    return tuple(a.reshape(rows, 1, cells) for a in outs)


def solution(mesh):
    in_specs = (
        P("strike", "cross", None),
        P("strike", "cross", None),
        P("strike", "cross", None),
        P(),
    )
    out_specs = (P("strike", "cross", None), P("strike", "cross", None))
    return jax.shard_map(
        per_device, mesh=mesh, in_specs=in_specs, out_specs=out_specs, check_vma=False
    )
```

```python
import functools
import math

import jax
import jax.numpy as jnp
from jax import lax
from jax.experimental import pallas as pl
from jax.experimental.pallas import tpu as pltpu
from jax.sharding import PartitionSpec as P

CLASSES = 8
DEFECT = 2
SWEEPS = 3

STORE = 0.5
LOW = 0.05
HIGH = 1.95

SUB = 8
LANES = 128
HALF = LANES // 2
MESH = pl.DeviceIdType.MESH


def chebyshev_weights(count):
    middle = 0.5 * (LOW + HIGH)
    half = 0.5 * (HIGH - LOW)
    return [
        1.0 / (middle + half * math.cos(math.pi * (2 * j + 1) / (2 * count))) for j in range(count)
    ]


def power(x, count):
    result = None
    while count:
        if count & 1:
            result = x if result is None else result * x
        count >>= 1
        if count:
            x = x * x
    return result


def kernel(
    crosses, strikes, dips, pressure, facies, source, table, out_p, out_d, x, fac, halo, halo_fac,
    rims, mob, res, ans, part, qpow, full, col, rim_ans, rim_base, far_box, far_out,
    cross_sems, halo_sems, rim_sems, far_sems, out_sems,
):
    tiles, width = x.shape[2], x.shape[4]
    main = width - LANES
    rows = tiles * SUB
    pieces = 2 if crosses % 2 == 0 else 1
    piece = crosses // pieces
    cross = lax.axis_index("cross")
    strike = lax.axis_index("strike")

    def across(k):
        return lax.rem(cross + k, crosses)

    def before(k):
        return lax.rem(cross + crosses - k, crosses)

    up = lax.rem(strike + 1, strikes)
    down = lax.rem(strike + strikes - 1, strikes)

    def peer_of(k):
        return (cross, lax.rem(strike + k, strikes))

    barrier = pltpu.get_barrier_semaphore()
    peers = [(across(k), strike) for k in range(1, crosses)]
    peers += [(cross, up), (cross, down)]
    peers += [peer_of(k) for k in range(1, strikes)]
    for peer in peers:
        pl.semaphore_signal(barrier, inc=1, device_id=peer, device_id_type=MESH)

    def send(src, dst, sems, where, target, k):
        if k == 0:
            return pltpu.make_async_copy(src, dst, sems.at[(1,) + where])
        return pltpu.make_async_remote_copy(
            src_ref=src,
            dst_ref=dst,
            send_sem=sems.at[(0,) + where],
            recv_sem=sems.at[(1,) + where],
            device_id=target,
            device_id_type=MESH,
        )

    def arrived(ref, sems, where, target, k):
        copy = send(ref, ref, sems, where, target, k)
        if k == 0:
            copy.wait()
        else:
            copy.wait_recv()

    def landing(f, c):
        if f == 1:
            return fac.at[c, :, :, pl.ds(0, main)], halo_fac.at[c]
        return x.at[c, f, :, :, pl.ds(0, main)], halo.at[c, f // 2]

    def columns(start, size):
        return pl.ds(pl.multiple_of(start, LANES), size)

    raws = (pressure, facies, source)

    def deal(k):
        to = across(k)
        after = lax.rem(to + 1, crosses) * main
        ahead = lax.rem(to + crosses - 1, crosses) * main + main - LANES
        for f in range(3):
            body, edge = landing(f, cross)
            for t in range(tiles):
                send(
                    raws[f].at[:, t, 0, columns(to * main, main)], body.at[t],
                    cross_sems, (f, k), (to, strike), k,
                ).start()
            for t in range(tiles):
                for side, begin in ((0, after), (1, ahead)):
                    send(
                        raws[f].at[:, t, 0, columns(begin, LANES)], edge.at[side, t],
                        halo_sems, (f, k), (to, strike), k,
                    ).start()

    def dealt(f):
        for k in range(crosses):
            body, edge = landing(f, before(k))
            arrived(body, cross_sems, (f, k), (across(k), strike), k)
            arrived(edge, halo_sems, (f, k), (across(k), strike), k)

    deal(0)
    pl.semaphore_wait(barrier, len(peers))
    for k in range(1, crosses):
        deal(k)
    dealt(0)
    dealt(1)

    inside = (strike > 0, strike < strikes - 1)
    lane = lax.broadcasted_iota(jnp.int32, (1, 1, width), 2)
    valid = (
        (lane < main)
        | ((lane < main + HALF) & (cross < crosses - 1))
        | ((lane >= main + HALF) & (cross > 0))
    )
    sub = lax.broadcasted_iota(jnp.int32, (1, SUB, width), 1)
    none = jnp.zeros((1, SUB, width), jnp.float32)
    tip = lax.broadcasted_iota(jnp.int32, (crosses, SUB, LANES), 2) < HALF
    real = valid[:, :, main:]

    def classed(codes):
        base = jnp.zeros(codes.shape, jnp.float32)
        for code in range(CLASSES):
            base = jnp.where(codes == code, table[code], base)
        return base

    def joined(f):
        for t in range(tiles):
            merged = jnp.where(tip, halo[:, f // 2, 0, t], halo[:, f // 2, 1, t])
            x[:, f, t, :, main:] = jnp.where(real, merged, 0.0)

    joined(0)
    for t in range(tiles):
        merged = classed(jnp.where(tip, halo_fac[:, 0, t], halo_fac[:, 1, t]))
        x[:, 1, t, :, main:] = jnp.where(real, merged, 0.0)
        x[:, 1, t, :, :main] = classed(fac[:, t, :, :main])

    rim_copies = [
        send(
            x.at[:, pl.ds(0, 2), tile, pl.ds(row, 1), :], rims.at[side],
            rim_sems, (side,), (cross, target), 1,
        )
        for side, target, tile, row in ((0, up, tiles - 1, SUB - 1), (1, down, 0, 0))
    ]
    for copy in rim_copies:
        copy.start()

    def finals(which, blocks):
        ref = out_p if which == 0 else out_d
        copies = []
        for k in reversed(range(crosses)):
            to = across(k)
            for t in blocks:
                src = x.at[to, 0, t] if which == 0 else res.at[to, t]
                copies.append(
                    send(
                        src.at[:, pl.ds(0, main)],
                        ref.at[:, t, 0, columns(cross * main, main)],
                        out_sems, (which, k), (to, strike), k,
                    )
                )
        return copies

    def left(a):
        return pltpu.roll(a, 1, 2)

    def right(a):
        return pltpu.roll(a, width - 1, 2)

    def later(a, k):
        return pltpu.roll(a, k, 1)

    def sooner(a, k):
        return pltpu.roll(a, SUB - k, 1)

    def mobility(base, p):
        return base * (1.0 + 0.5 * jnp.tanh(p))

    def trade(parity, which, low, size):
        def box(a):
            return far_box.at[parity, a, pl.ds(low, size)]

        copies = []
        for k in range(1, strikes):
            row = far_out.at[parity, lax.div(strike + k, strikes), pl.ds(low, size)]
            copy = send(row, box(strike), far_sems, (parity, which, k - 1), peer_of(k), k)
            copy.start()
            copies.append(copy)

        def finish():
            for k in range(1, strikes):
                origin = lax.rem(strike + strikes - k, strikes)
                arrived(box(origin), far_sems, (parity, which, k - 1), peer_of(k), k)

        def settle():
            for copy in copies:
                copy.wait_send()

        return finish, settle

    omega = chebyshev_weights(SWEEPS)

    def one_step(step, carry):
        turn = step * (SWEEPS + 1)
        parity = lax.rem(turn, 2)
        total = jnp.zeros((crosses, SUB, width), jnp.float32)
        for t in range(tiles):
            m = mobility(x[:, 1, t], x[:, 0, t])
            mob[t] = m
            total = total + m
        total = jnp.sum(total, axis=1, keepdims=True)
        far_out[parity, 0] = total
        far_out[parity, 1] = total
        far_box[parity, strike] = total
        finish, settle = trade(parity, 0, 0, crosses)

        @pl.when(step == 0)
        def _():
            for copy in rim_copies:
                copy.wait_recv()
            for copy in rim_copies:
                copy.wait_send()
            for side in range(2):
                rim_ans[side, 1] = jnp.where(inside[side], rims[side, :, 0], 0.0)
                rim_base[side] = jnp.where(inside[side], rims[side, :, 1], 0.0)
            dealt(2)
            joined(2)

        rim_p = [rim_ans[side, 1] for side in range(2)]
        rim_m = [mobility(rim_base[side], rim_p[side]) for side in range(2)]
        first_p, first_m = x[:, 0, 0], mob[0]
        last_p, last_m = x[:, 0, tiles - 1], mob[tiles - 1]
        p_was = jnp.where(sub == 0, rim_p[0], later(last_p, 1))
        m_was = jnp.where(sub == 0, rim_m[0], later(last_m, 1))
        p, m = first_p, first_m
        flux = 0.5 * (m + m_was) * (p - p_was)
        for t in range(tiles):
            if t + 1 < tiles:
                p_next, m_next = x[:, 0, t + 1], mob[t + 1]
            else:
                p_next = jnp.where(sub == SUB - 1, rim_p[1], sooner(first_p, 1))
                m_next = jnp.where(sub == SUB - 1, rim_m[1], sooner(first_m, 1))
            flux_next = 0.5 * (m_next + m) * (p_next - p)
            along = 0.5 * (m + left(m)) * (p - left(p))
            p_wide = jnp.concatenate([none, p, none], axis=0)
            m_wide = jnp.concatenate([none, m, none], axis=0)
            over = 0.5 * (m_wide[1:] + m_wide[:-1]) * (p_wide[1:] - p_wide[:-1])
            applied = STORE * p + (flux - flux_next) + (along - right(along)) + (over[:-1] - over[1:])
            res[:, t] = jnp.where(valid, x[:, 2, t] - applied, 0.0)
            ans[t] = jnp.zeros_like(p)
            p, m, flux = p_next, m_next, flux_next

        @pl.when(step == DEFECT - 1)
        def _():
            for copy in finals(1, range(tiles)):
                copy.start()

        finish()
        settle()
        total = far_box[parity, 0]
        for a in range(1, strikes):
            total = total + far_box[parity, a]
        mref = total * (1.0 / dips)

        root = jnp.sqrt((STORE + 4.0 * mref) * (STORE + 8.0 * mref))
        q = 2.0 * mref / (STORE + 6.0 * mref + root)
        gain = 1.0 / root
        chunk = power(q, tiles)
        block = power(q, rows)
        whole = power(block, strikes)
        unmirror = 1.0 / (1.0 - whole * whole)
        mirror_up = jnp.ones_like(q)
        mirror_down = mirror_up
        twice = block * block
        for a in range(strikes - 1):
            mirror_up = jnp.where(a < strike, mirror_up * twice, mirror_up)
            mirror_down = jnp.where(a < strikes - 1 - strike, mirror_down * twice, mirror_down)
        for i, value in enumerate((chunk, block, unmirror, mirror_up, mirror_down)):
            col[i] = value
        spread = (crosses, SUB, width)
        for i, value in enumerate((mref, q, gain)):
            full[i] = jnp.broadcast_to(value, spread)
        running = q
        for t in range(tiles):
            qpow[t] = jnp.broadcast_to(running, spread)
            running = running * q
        ahead = jnp.ones((crosses, SUB, width), jnp.float32)
        behind = ahead
        step_up = jnp.broadcast_to(chunk, ahead.shape)
        for bit in (1, 2, 4):
            ahead = jnp.where((sub & bit) != 0, ahead * step_up, ahead)
            behind = jnp.where((sub & bit) == 0, behind * step_up, behind)
            step_up = step_up * step_up
        part[0], part[1] = ahead, behind
        for side in range(2):
            rim_ans[side, 0] = jnp.zeros((crosses, 1, width), jnp.float32)

        def sweep(j, carry):
            parity = lax.rem(turn + 1 + j, 2)
            weight = jnp.float32(omega[0])
            for i in range(1, SWEEPS):
                weight = jnp.where(j == i, jnp.float32(omega[i]), weight)
            keep = 1.0 - weight
            waiting = []
            for which in range(pieces):
                low, high = which * piece, (which + 1) * piece
                mref, q, chunk = full[0, low:high], full[1, low:high], col[0, low:high]
                y = jnp.zeros((piece, SUB, width), jnp.float32)
                for t in range(tiles):
                    u = ans[t, low:high]
                    near = left(u) + right(u)
                    if low > 0:
                        near = near + ans[t, low - 1 : high - 1]
                    elif piece > 1:
                        near = near + jnp.concatenate([none, u[:-1]], axis=0)
                    if high < crosses:
                        near = near + ans[t, low + 1 : high + 1]
                    elif piece > 1:
                        near = near + jnp.concatenate([u[1:], none], axis=0)
                    r = res[low:high, t] + mref * near
                    mob[t, low:high] = r
                    y = q * y
                    part[2 + t, low:high] = y
                    y = r + y
                z = jnp.zeros((piece, SUB, width), jnp.float32)
                for t in reversed(range(tiles)):
                    z = mob[t, low:high] + q * z
                    part[2 + t, low:high] = part[2 + t, low:high] + z
                step_up = chunk
                for k in (1, 2, 4):
                    y = y + step_up * jnp.where(sub >= k, later(y, k), 0.0)
                    z = z + step_up * jnp.where(sub < SUB - k, sooner(z, k), 0.0)
                    step_up = step_up * step_up
                tail, head = y[:, SUB - 1 :, :], z[:, :1, :]
                block = col[1, low:high]
                far_out[parity, 0, low:high] = tail + col[3, low:high] * block * head
                far_out[parity, 1, low:high] = head + col[4, low:high] * block * tail
                waiting.append((y, z, tail, head) + trade(parity, which, low, piece))

            for which in range(pieces):
                low, high = which * piece, (which + 1) * piece
                y, z, tail, head, finish, settle = waiting[which]
                block, unmirror = col[1, low:high], col[2, low:high]
                mirror_up, mirror_down = col[3, low:high], col[4, low:high]
                thin_q = full[1, low:high, :1, :]
                scale = weight * full[2, low:high]
                thin_scale = weight * full[2, low:high, :1, :]
                upward = far_out[parity, 0, low:high]
                downward = far_out[parity, 1, low:high]
                finish()
                from_left = jnp.zeros_like(upward)
                from_right = jnp.zeros_like(upward)
                for a in range(strikes - 1):
                    b = strikes - 1 - a
                    from_left = jnp.where(
                        a < strike, from_left * block + far_box[parity, a, low:high], from_left
                    )
                    from_right = jnp.where(
                        b > strike, from_right * block + far_box[parity, b, low:high], from_right
                    )
                from_left, from_right = (
                    (from_left + mirror_up * (from_right * block + downward)) * unmirror,
                    (from_right + mirror_down * (from_left * block + upward)) * unmirror,
                )
                rim_ans[0, 0, low:high] = keep * rim_ans[0, 0, low:high] + thin_scale * (
                    from_left + thin_q * (head + block * from_right)
                )
                rim_ans[1, 0, low:high] = keep * rim_ans[1, 0, low:high] + thin_scale * (
                    from_right + thin_q * (tail + block * from_left)
                )
                y = jnp.where(sub >= 1, later(y, 1), 0.0) + part[0, low:high] * from_left
                z = jnp.where(sub < SUB - 1, sooner(z, 1), 0.0) + part[1, low:high] * from_right
                for t in range(tiles):
                    solved = part[2 + t, low:high] + (
                        qpow[t, low:high] * y + qpow[tiles - 1 - t, low:high] * z
                    )
                    ans[t, low:high] = keep * ans[t, low:high] + scale * solved
            for which in range(pieces):
                waiting[which][5]()
            return carry

        lax.fori_loop(0, SWEEPS, sweep, 0)
        for t in range(tiles):
            x[:, 0, t] = x[:, 0, t] + ans[t]

            @pl.when(step == DEFECT - 1)
            def _(t=t):
                for copy in finals(0, [t]):
                    copy.start()

        for side in range(2):
            rim_ans[side, 1] = rim_ans[side, 1] + jnp.where(inside[side], rim_ans[side, 0], 0.0)
        return carry

    lax.fori_loop(0, DEFECT, one_step, 0)

    for which in (1, 0):
        ref = out_p if which == 0 else out_d
        for k in range(crosses):
            to, frm = across(k), before(k)
            arrived(
                ref.at[:, :, 0, columns(frm * main, main)], out_sems, (which, k), (to, strike), k
            )
    for k in range(1, crosses):
        to = across(k)
        for f in range(3):
            body, edge = landing(f, cross)
            send(body, body, cross_sems, (f, k), (to, strike), k).wait_send()
            send(edge, edge, halo_sems, (f, k), (to, strike), k).wait_send()
        for which in range(2):
            src = x.at[to, 0] if which == 0 else res.at[to]
            src = src.at[:, :, pl.ds(0, main)]
            send(src, src, out_sems, (which, k), (to, strike), k).wait_send()


def per_device(pressure, source, facies, mobility_table):
    crosses = lax.axis_size("cross")
    strikes = lax.axis_size("strike")
    rows, _, cells = pressure.shape
    tiles = rows // SUB
    main = cells // crosses
    width = main + LANES

    def dealt(a):
        return a.reshape(SUB, tiles, 1, cells)

    f32 = jnp.float32
    vm = pltpu.VMEM
    dma = pltpu.SemaphoreType.DMA
    full = (crosses, SUB, width)
    field = (tiles,) + full
    thin = (crosses, 1, width)
    whole = jax.ShapeDtypeStruct((SUB, tiles, 1, cells), f32)
    anywhere = pl.BlockSpec(memory_space=pltpu.HBM)
    outs = pl.pallas_call(
        functools.partial(kernel, crosses, strikes, rows * strikes),
        out_shape=[whole, whole],
        in_specs=[anywhere] * 3 + [pl.BlockSpec(memory_space=pltpu.SMEM)],
        out_specs=[anywhere] * 2,
        scratch_shapes=[
            vm((crosses, 3, tiles, SUB, width), f32),
            vm((crosses, tiles, SUB, width), jnp.int32),
            vm((crosses, 2, 2, tiles, SUB, LANES), f32),
            vm((crosses, 2, tiles, SUB, LANES), jnp.int32),
            vm((2, crosses, 2, 1, width), f32),
            vm(field, f32),
            vm((crosses, tiles, SUB, width), f32),
            vm(field, f32),
            vm((tiles + 2,) + full, f32),
            vm(field, f32),
            vm((3,) + full, f32),
            vm((5,) + thin, f32),
            vm((2, 2) + thin, f32),
            vm((2,) + thin, f32),
            vm((2, strikes) + thin, f32),
            vm((2, 2) + thin, f32),
            dma((2, 3, crosses)),
            dma((2, 3, crosses)),
            dma((2, 2)),
            dma((2, 2, 2, max(strikes - 1, 1))),
            dma((2, 2, crosses)),
        ],
        compiler_params=pltpu.CompilerParams(
            collective_id=0, has_side_effects=True, vmem_limit_bytes=60 * 1024 * 1024
        ),
    )(dealt(pressure), dealt(facies), dealt(source), mobility_table)
    return tuple(a.reshape(rows, 1, cells) for a in outs)


def solution(mesh):
    in_specs = (
        P("strike", "cross", None),
        P("strike", "cross", None),
        P("strike", "cross", None),
        P(),
    )
    out_specs = (P("strike", "cross", None), P("strike", "cross", None))
    return jax.shard_map(
        per_device, mesh=mesh, in_specs=in_specs, out_specs=out_specs, check_vma=False
    )
```

```python
import functools
import math

import jax
import jax.numpy as jnp
from jax import lax
from jax.experimental import pallas as pl
from jax.experimental.pallas import tpu as pltpu
from jax.sharding import PartitionSpec as P

CLASSES = 8
DEFECT = 2
SWEEPS = 3

STORE = 0.5
LOW = 0.05
HIGH = 1.95

SUB = 8
LANES = 128
HALF = LANES // 2
MESH = pl.DeviceIdType.MESH


def chebyshev_weights(count):
    middle = 0.5 * (LOW + HIGH)
    half = 0.5 * (HIGH - LOW)
    return [
        1.0 / (middle + half * math.cos(math.pi * (2 * j + 1) / (2 * count))) for j in range(count)
    ]


def power(x, count):
    result = None
    while count:
        if count & 1:
            result = x if result is None else result * x
        count >>= 1
        if count:
            x = x * x
    return result


def kernel(
    crosses, strikes, dips, pressure, facies, source, table, out_p, out_d, x, fac, halo, halo_fac,
    rims, mob, res, ans, part, qpow, full, col, rim_ans, rim_base, far_box, far_out,
    cross_sems, halo_sems, rim_sems, far_sems, out_sems,
):
    tiles, width = x.shape[2], x.shape[4]
    main = width - LANES
    rows = tiles * SUB
    pieces = 2 if crosses % 2 == 0 else 1
    piece = crosses // pieces
    cross = lax.axis_index("cross")
    strike = lax.axis_index("strike")

    def across(k):
        return lax.rem(cross + k, crosses)

    def before(k):
        return lax.rem(cross + crosses - k, crosses)

    up = lax.rem(strike + 1, strikes)
    down = lax.rem(strike + strikes - 1, strikes)

    def peer_of(k):
        return (cross, lax.rem(strike + k, strikes))

    barrier = pltpu.get_barrier_semaphore()
    peers = [(across(k), strike) for k in range(1, crosses)]
    peers += [(cross, up), (cross, down)]
    peers += [peer_of(k) for k in range(1, strikes)]
    for peer in peers:
        pl.semaphore_signal(barrier, inc=1, device_id=peer, device_id_type=MESH)

    def send(src, dst, sems, where, target, k):
        if k == 0:
            return pltpu.make_async_copy(src, dst, sems.at[(1,) + where])
        return pltpu.make_async_remote_copy(
            src_ref=src,
            dst_ref=dst,
            send_sem=sems.at[(0,) + where],
            recv_sem=sems.at[(1,) + where],
            device_id=target,
            device_id_type=MESH,
        )

    def arrived(ref, sems, where, target, k):
        copy = send(ref, ref, sems, where, target, k)
        if k == 0:
            copy.wait()
        else:
            copy.wait_recv()

    def landing(f, c):
        if f == 1:
            return fac.at[c, :, :, pl.ds(0, main)], halo_fac.at[c]
        return x.at[c, f, :, :, pl.ds(0, main)], halo.at[c, f // 2]

    def columns(start, size):
        return pl.ds(pl.multiple_of(start, LANES), size)

    raws = (pressure, facies, source)

    def deal(k):
        to = across(k)
        after = lax.rem(to + 1, crosses) * main
        ahead = lax.rem(to + crosses - 1, crosses) * main + main - LANES
        for f in range(3):
            body, edge = landing(f, cross)
            for t in range(tiles):
                send(
                    raws[f].at[:, t, 0, columns(to * main, main)], body.at[t],
                    cross_sems, (f, k), (to, strike), k,
                ).start()
            for t in range(tiles):
                for side, begin in ((0, after), (1, ahead)):
                    send(
                        raws[f].at[:, t, 0, columns(begin, LANES)], edge.at[side, t],
                        halo_sems, (f, k), (to, strike), k,
                    ).start()

    def dealt(f):
        for k in range(crosses):
            body, edge = landing(f, before(k))
            arrived(body, cross_sems, (f, k), (across(k), strike), k)
            arrived(edge, halo_sems, (f, k), (across(k), strike), k)

    deal(0)
    pl.semaphore_wait(barrier, len(peers))
    for k in range(1, crosses):
        deal(k)
    dealt(0)
    dealt(1)

    inside = (strike > 0, strike < strikes - 1)
    lane = lax.broadcasted_iota(jnp.int32, (1, 1, width), 2)
    valid = (
        (lane < main)
        | ((lane < main + HALF) & (cross < crosses - 1))
        | ((lane >= main + HALF) & (cross > 0))
    )
    sub = lax.broadcasted_iota(jnp.int32, (1, SUB, width), 1)
    none = jnp.zeros((1, SUB, width), jnp.float32)
    tip = lax.broadcasted_iota(jnp.int32, (crosses, SUB, LANES), 2) < HALF
    real = valid[:, :, main:]

    def classed(codes):
        base = jnp.zeros(codes.shape, jnp.float32)
        for code in range(CLASSES):
            base = jnp.where(codes == code, table[code], base)
        return base

    def joined(f):
        for t in range(tiles):
            merged = jnp.where(tip, halo[:, f // 2, 0, t], halo[:, f // 2, 1, t])
            x[:, f, t, :, main:] = jnp.where(real, merged, 0.0)

    joined(0)
    for t in range(tiles):
        merged = classed(jnp.where(tip, halo_fac[:, 0, t], halo_fac[:, 1, t]))
        x[:, 1, t, :, main:] = jnp.where(real, merged, 0.0)
        x[:, 1, t, :, :main] = classed(fac[:, t, :, :main])

    rim_copies = [
        send(
            x.at[:, pl.ds(0, 2), tile, pl.ds(row, 1), :], rims.at[side],
            rim_sems, (side,), (cross, target), 1,
        )
        for side, target, tile, row in ((0, up, tiles - 1, SUB - 1), (1, down, 0, 0))
    ]
    for copy in rim_copies:
        copy.start()

    def finals(which):
        ref = out_p if which == 0 else out_d
        copies = []
        for k in reversed(range(crosses)):
            to = across(k)
            for t in range(tiles):
                src = x.at[to, 0, t] if which == 0 else res.at[to, t]
                copies.append(
                    send(
                        src.at[:, pl.ds(0, main)],
                        ref.at[:, t, 0, columns(cross * main, main)],
                        out_sems, (which, k), (to, strike), k,
                    )
                )
        return copies

    def left(a):
        return pltpu.roll(a, 1, 2)

    def right(a):
        return pltpu.roll(a, width - 1, 2)

    def later(a, k):
        return pltpu.roll(a, k, 1)

    def sooner(a, k):
        return pltpu.roll(a, SUB - k, 1)

    def mobility(base, p):
        return base * (1.0 + 0.5 * jnp.tanh(p))

    def trade(parity, which, low, size):
        def box(a):
            return far_box.at[parity, a, pl.ds(low, size)]

        copies = []
        for k in range(1, strikes):
            row = far_out.at[parity, lax.div(strike + k, strikes), pl.ds(low, size)]
            copy = send(row, box(strike), far_sems, (parity, which, k - 1), peer_of(k), k)
            copy.start()
            copies.append(copy)

        def finish():
            for k in range(1, strikes):
                origin = lax.rem(strike + strikes - k, strikes)
                arrived(box(origin), far_sems, (parity, which, k - 1), peer_of(k), k)

        def settle():
            for copy in copies:
                copy.wait_send()

        return finish, settle

    omega = chebyshev_weights(SWEEPS)

    def one_step(step, carry):
        turn = step * (SWEEPS + 1)
        parity = lax.rem(turn, 2)
        total = jnp.zeros((crosses, SUB, width), jnp.float32)
        for t in range(tiles):
            m = mobility(x[:, 1, t], x[:, 0, t])
            mob[t] = m
            total = total + m
        total = jnp.sum(total, axis=1, keepdims=True)
        far_out[parity, 0] = total
        far_out[parity, 1] = total
        far_box[parity, strike] = total
        finish, settle = trade(parity, 0, 0, crosses)

        @pl.when(step == 0)
        def _():
            for copy in rim_copies:
                copy.wait_recv()
            for copy in rim_copies:
                copy.wait_send()
            for side in range(2):
                rim_ans[side, 1] = jnp.where(inside[side], rims[side, :, 0], 0.0)
                rim_base[side] = jnp.where(inside[side], rims[side, :, 1], 0.0)
            dealt(2)
            joined(2)

        rim_p = [rim_ans[side, 1] for side in range(2)]
        rim_m = [mobility(rim_base[side], rim_p[side]) for side in range(2)]
        first_p, first_m = x[:, 0, 0], mob[0]
        last_p, last_m = x[:, 0, tiles - 1], mob[tiles - 1]
        p_was = jnp.where(sub == 0, rim_p[0], later(last_p, 1))
        m_was = jnp.where(sub == 0, rim_m[0], later(last_m, 1))
        p, m = first_p, first_m
        flux = 0.5 * (m + m_was) * (p - p_was)
        for t in range(tiles):
            if t + 1 < tiles:
                p_next, m_next = x[:, 0, t + 1], mob[t + 1]
            else:
                p_next = jnp.where(sub == SUB - 1, rim_p[1], sooner(first_p, 1))
                m_next = jnp.where(sub == SUB - 1, rim_m[1], sooner(first_m, 1))
            flux_next = 0.5 * (m_next + m) * (p_next - p)
            along = 0.5 * (m + left(m)) * (p - left(p))
            p_wide = jnp.concatenate([none, p, none], axis=0)
            m_wide = jnp.concatenate([none, m, none], axis=0)
            over = 0.5 * (m_wide[1:] + m_wide[:-1]) * (p_wide[1:] - p_wide[:-1])
            applied = STORE * p + (flux - flux_next) + (along - right(along)) + (over[:-1] - over[1:])
            res[:, t] = jnp.where(valid, x[:, 2, t] - applied, 0.0)
            ans[t] = jnp.zeros_like(p)
            p, m, flux = p_next, m_next, flux_next

        @pl.when(step == DEFECT - 1)
        def _():
            for copy in finals(1):
                copy.start()

        finish()
        settle()
        total = far_box[parity, 0]
        for a in range(1, strikes):
            total = total + far_box[parity, a]
        mref = total * (1.0 / dips)

        root = jnp.sqrt((STORE + 4.0 * mref) * (STORE + 8.0 * mref))
        q = 2.0 * mref / (STORE + 6.0 * mref + root)
        gain = 1.0 / root
        chunk = power(q, tiles)
        block = power(q, rows)
        whole = power(block, strikes)
        unmirror = 1.0 / (1.0 - whole * whole)
        mirror_up = jnp.ones_like(q)
        mirror_down = mirror_up
        twice = block * block
        for a in range(strikes - 1):
            mirror_up = jnp.where(a < strike, mirror_up * twice, mirror_up)
            mirror_down = jnp.where(a < strikes - 1 - strike, mirror_down * twice, mirror_down)
        for i, value in enumerate((chunk, block, unmirror, mirror_up, mirror_down)):
            col[i] = value
        spread = (crosses, SUB, width)
        for i, value in enumerate((mref, q, gain)):
            full[i] = jnp.broadcast_to(value, spread)
        running = q
        for t in range(tiles):
            qpow[t] = jnp.broadcast_to(running, spread)
            running = running * q
        ahead = jnp.ones((crosses, SUB, width), jnp.float32)
        behind = ahead
        step_up = jnp.broadcast_to(chunk, ahead.shape)
        for bit in (1, 2, 4):
            ahead = jnp.where((sub & bit) != 0, ahead * step_up, ahead)
            behind = jnp.where((sub & bit) == 0, behind * step_up, behind)
            step_up = step_up * step_up
        part[0], part[1] = ahead, behind
        for side in range(2):
            rim_ans[side, 0] = jnp.zeros((crosses, 1, width), jnp.float32)

        def sweep(j, carry):
            parity = lax.rem(turn + 1 + j, 2)
            weight = jnp.float32(omega[0])
            for i in range(1, SWEEPS):
                weight = jnp.where(j == i, jnp.float32(omega[i]), weight)
            keep = 1.0 - weight
            waiting = []
            for which in range(pieces):
                low, high = which * piece, (which + 1) * piece
                mref, q, chunk = full[0, low:high], full[1, low:high], col[0, low:high]
                y = jnp.zeros((piece, SUB, width), jnp.float32)
                for t in range(tiles):
                    u = ans[t, low:high]
                    near = left(u) + right(u)
                    if low > 0:
                        near = near + ans[t, low - 1 : high - 1]
                    elif piece > 1:
                        near = near + jnp.concatenate([none, u[:-1]], axis=0)
                    if high < crosses:
                        near = near + ans[t, low + 1 : high + 1]
                    elif piece > 1:
                        near = near + jnp.concatenate([u[1:], none], axis=0)
                    r = res[low:high, t] + mref * near
                    mob[t, low:high] = r
                    y = q * y
                    part[2 + t, low:high] = y
                    y = r + y
                z = jnp.zeros((piece, SUB, width), jnp.float32)
                for t in reversed(range(tiles)):
                    z = mob[t, low:high] + q * z
                    part[2 + t, low:high] = part[2 + t, low:high] + z
                step_up = chunk
                for k in (1, 2, 4):
                    y = y + step_up * jnp.where(sub >= k, later(y, k), 0.0)
                    z = z + step_up * jnp.where(sub < SUB - k, sooner(z, k), 0.0)
                    step_up = step_up * step_up
                tail, head = y[:, SUB - 1 :, :], z[:, :1, :]
                block = col[1, low:high]
                far_out[parity, 0, low:high] = tail + col[3, low:high] * block * head
                far_out[parity, 1, low:high] = head + col[4, low:high] * block * tail
                waiting.append((y, z, tail, head) + trade(parity, which, low, piece))

            for which in range(pieces):
                low, high = which * piece, (which + 1) * piece
                y, z, tail, head, finish, settle = waiting[which]
                block, unmirror = col[1, low:high], col[2, low:high]
                mirror_up, mirror_down = col[3, low:high], col[4, low:high]
                thin_q = full[1, low:high, :1, :]
                scale = weight * full[2, low:high]
                thin_scale = weight * full[2, low:high, :1, :]
                upward = far_out[parity, 0, low:high]
                downward = far_out[parity, 1, low:high]
                finish()
                from_left = jnp.zeros_like(upward)
                from_right = jnp.zeros_like(upward)
                for a in range(strikes - 1):
                    b = strikes - 1 - a
                    from_left = jnp.where(
                        a < strike, from_left * block + far_box[parity, a, low:high], from_left
                    )
                    from_right = jnp.where(
                        b > strike, from_right * block + far_box[parity, b, low:high], from_right
                    )
                from_left, from_right = (
                    (from_left + mirror_up * (from_right * block + downward)) * unmirror,
                    (from_right + mirror_down * (from_left * block + upward)) * unmirror,
                )
                rim_ans[0, 0, low:high] = keep * rim_ans[0, 0, low:high] + thin_scale * (
                    from_left + thin_q * (head + block * from_right)
                )
                rim_ans[1, 0, low:high] = keep * rim_ans[1, 0, low:high] + thin_scale * (
                    from_right + thin_q * (tail + block * from_left)
                )
                y = jnp.where(sub >= 1, later(y, 1), 0.0) + part[0, low:high] * from_left
                z = jnp.where(sub < SUB - 1, sooner(z, 1), 0.0) + part[1, low:high] * from_right
                for t in range(tiles):
                    solved = part[2 + t, low:high] + (
                        qpow[t, low:high] * y + qpow[tiles - 1 - t, low:high] * z
                    )
                    ans[t, low:high] = keep * ans[t, low:high] + scale * solved
            for which in range(pieces):
                waiting[which][5]()
            return carry

        lax.fori_loop(0, SWEEPS, sweep, 0)
        for t in range(tiles):
            x[:, 0, t] = x[:, 0, t] + ans[t]
        for side in range(2):
            rim_ans[side, 1] = rim_ans[side, 1] + jnp.where(inside[side], rim_ans[side, 0], 0.0)
        return carry

    lax.fori_loop(0, DEFECT, one_step, 0)

    for copy in finals(0):
        copy.start()
    for which in (1, 0):
        ref = out_p if which == 0 else out_d
        for k in range(crosses):
            to, frm = across(k), before(k)
            arrived(
                ref.at[:, :, 0, columns(frm * main, main)], out_sems, (which, k), (to, strike), k
            )
    for k in range(1, crosses):
        to = across(k)
        for f in range(3):
            body, edge = landing(f, cross)
            send(body, body, cross_sems, (f, k), (to, strike), k).wait_send()
            send(edge, edge, halo_sems, (f, k), (to, strike), k).wait_send()
        for which in range(2):
            src = x.at[to, 0] if which == 0 else res.at[to]
            src = src.at[:, :, pl.ds(0, main)]
            send(src, src, out_sems, (which, k), (to, strike), k).wait_send()


def per_device(pressure, source, facies, mobility_table):
    crosses = lax.axis_size("cross")
    strikes = lax.axis_size("strike")
    rows, _, cells = pressure.shape
    tiles = rows // SUB
    main = cells // crosses
    width = main + LANES

    def dealt(a):
        return a.reshape(SUB, tiles, 1, cells)

    f32 = jnp.float32
    vm = pltpu.VMEM
    dma = pltpu.SemaphoreType.DMA
    full = (crosses, SUB, width)
    field = (tiles,) + full
    thin = (crosses, 1, width)
    whole = jax.ShapeDtypeStruct((SUB, tiles, 1, cells), f32)
    anywhere = pl.BlockSpec(memory_space=pltpu.HBM)
    outs = pl.pallas_call(
        functools.partial(kernel, crosses, strikes, rows * strikes),
        out_shape=[whole, whole],
        in_specs=[anywhere] * 3 + [pl.BlockSpec(memory_space=pltpu.SMEM)],
        out_specs=[anywhere] * 2,
        scratch_shapes=[
            vm((crosses, 3, tiles, SUB, width), f32),
            vm((crosses, tiles, SUB, width), jnp.int32),
            vm((crosses, 2, 2, tiles, SUB, LANES), f32),
            vm((crosses, 2, tiles, SUB, LANES), jnp.int32),
            vm((2, crosses, 2, 1, width), f32),
            vm(field, f32),
            vm((crosses, tiles, SUB, width), f32),
            vm(field, f32),
            vm((tiles + 2,) + full, f32),
            vm(field, f32),
            vm((3,) + full, f32),
            vm((5,) + thin, f32),
            vm((2, 2) + thin, f32),
            vm((2,) + thin, f32),
            vm((2, strikes) + thin, f32),
            vm((2, 2) + thin, f32),
            dma((2, 3, crosses)),
            dma((2, 3, crosses)),
            dma((2, 2)),
            dma((2, 2, 2, max(strikes - 1, 1))),
            dma((2, 2, crosses)),
        ],
        compiler_params=pltpu.CompilerParams(
            collective_id=0, has_side_effects=True, vmem_limit_bytes=60 * 1024 * 1024
        ),
    )(dealt(pressure), dealt(facies), dealt(source), mobility_table)
    return tuple(a.reshape(rows, 1, cells) for a in outs)


def solution(mesh):
    in_specs = (
        P("strike", "cross", None),
        P("strike", "cross", None),
        P("strike", "cross", None),
        P(),
    )
    out_specs = (P("strike", "cross", None), P("strike", "cross", None))
    return jax.shard_map(
        per_device, mesh=mesh, in_specs=in_specs, out_specs=out_specs, check_vma=False
    )
```
